32 devices in a mesh: tile: 8 (over z, x), chan: 4 (over y, core).
Axes of the slice: x: 2, y: 2, z: 4, core: 2. Of those that a mesh axis runs over, the one named last changes fastest.
Arguments:
- features: bfloat16 [64, 64, 4096], P('tile', 'chan'), may hold values from -6 to 6
- conv_weight: bfloat16 [64, 576], P('chan'), may hold values from -0.25 to 0.25
- conv_bias: float32 [64], P('chan'), may hold values from -3 to 3
- down_weight: bfloat16 [64, 256], P(None, 'chan'), may hold values from -0.375 to 0.375
- cotangent: bfloat16 [16, 64, 4096], P('tile', 'chan'), may hold values from -0.0234375 to 0.0234375
- edge_links: int32 [64, 4], P('tile'), may hold values from 0 to 63, as said below
- edge_turns: int32 [64, 4], P('tile'), may hold values from 0 to 3
- corner_links: int32 [64, 4], P('tile'), may hold values from -1 to 63, as said below
- corner_turns: int32 [64, 4], P('tile'), may hold values from 0 to 3
- child_slot: int32 [64], P('tile'), may hold values from 0 to 63, as said below
Outputs:
- coarse: bfloat16 [16, 64, 4096], P('tile', 'chan')
- grad_conv: float32 [64, 576], P('chan')
- grad_bias: float32 [64], P('chan')
- grad_down: float32 [64, 256], P(None, 'chan')
The draws below stay inside these ranges and needn't reach their ends.
Inputs may be any that keep to these rules, and one draw needn't show every extreme that they name: `edge_links`: edge k: 0 north, 1 west, 2 south, 3 east. `corner_links`: corner k: 0 north-west, 1 south-west, 2 south-east, 3 north-east; -1 where no tile touches that corner. `child_slot`: a permutation of 0 to 63; coarse tile k lies on index k // 2 of tile; of the 8 fine tiles of one index of tile, at most 1 have their coarse tiles on any one index of tile, and that many do for some pair.
All inputs are finite; a program needn't handle non-finite values.
Results may differ from the reference program's by a relative error of at most 0.0055.
Values may be sent and summed in bfloat16 or wider, within the bound.
A program may use at most 64 MiB of HBM per device.

```python
import jax
import jax.numpy as jnp
from jax import lax

C = 64
S = 64
TILE_DEV = 8
TILES = 64
COARSE = 16
N_TILE = 8


def link_table(key, offsets, with_gaps):
    keys = jax.random.split(key, 4)
    position = jnp.arange(TILES, dtype=jnp.int32)[:, None]
    jitter = jax.random.randint(keys[0], (TILES, 4), -2, 3)
    local_links = (position + jnp.array(offsets, jnp.int32)[None, :] + jitter) % TILES
    far_links = jax.random.randint(keys[1], (TILES, 4), 0, TILES)
    far_pick = jax.random.randint(keys[2], (TILES, 4), 0, 8) == 0
    links = jnp.where(far_pick, far_links, local_links)
    if with_gaps:
        gap_pick = jax.random.randint(keys[3], (TILES, 4), 0, 16) == 0
        links = jnp.where(gap_pick, -1, links)
    return links.astype(jnp.int32)


def draw_edge_links(key, part):
    return link_table(jax.random.fold_in(key, 11), [-16, -1, 16, 1], False)


def draw_corner_links(key, part):
    return link_table(jax.random.fold_in(key, 23), [-17, 15, 17, -15], True)


def draw_child_slot(key, part):
    keys = jax.random.split(jax.random.fold_in(key, 37), 4)
    group_count = min(TILE_DEV, N_TILE)
    first_perm = jax.random.permutation(keys[0], N_TILE)
    second_perm = jax.random.permutation(keys[1], N_TILE)
    offsets = jax.random.permutation(keys[2], N_TILE)[:group_count]
    local_perm = jax.random.permutation(keys[3], TILE_DEV)
    tiles_all = jnp.arange(TILES, dtype=jnp.int32)
    device = tiles_all // TILE_DEV
    within = tiles_all % TILE_DEV
    owner_index = second_perm[(first_perm[device] + offsets[within % group_count]) % N_TILE]
    return (owner_index * TILE_DEV + local_perm[within]).astype(jnp.int32)


def plant(result, key, smallest, top_value):
    longest = result.shape.index(max(result.shape))
    spots = []
    for shift in (0, 1):
        where = [jax.random.randint(jax.random.fold_in(key, axis), (), 0, length) for axis, length in enumerate(result.shape)]
        where[longest] = (where[longest] + shift) % result.shape[longest]
        spots.append(tuple(where))
    return result.at[spots[0]].set(smallest).at[spots[1]].set(top_value)


def block_levels(rng, extent, shards, smallest, top_value):
    level = 1.0
    for dim, blocks in shards:
        heights = jax.random.uniform(jax.random.fold_in(jax.random.fold_in(rng, 6), dim), (blocks,), jnp.float32, smallest / len(shards), top_value / len(shards))
        level = level * jnp.repeat(jnp.exp(heights), extent[dim] // blocks).reshape((-1,) + (1,) * (len(extent) - 1 - dim))
    return level


def bell_draw(own_key, shape, scale, bound, cuts=(), kind=jnp.bfloat16):
    entries = scale * jax.random.normal(own_key, shape, jnp.float32)
    if cuts:
        entries = entries * block_levels(own_key, shape, cuts, -0.22, 0.18)
    return jnp.clip(entries, -bound, bound).astype(kind)


def setup_inputs(seed: int = 0) -> dict:
    key_of = jax.random.split(jax.random.key(seed), 11)
    return {
        "features": bell_draw(key_of[0], (TILES, C, S * S), 1.0, 6.0, ((0, 8), (1, 4))),
        "conv_weight": bell_draw(key_of[1], (C, C * 9), (C * 9) ** -0.5, 0.25, ((0, 4),)),
        "conv_bias": bell_draw(key_of[2], (C,), 0.5, 3.0, ((0, 4),), jnp.float32),
        "down_weight": bell_draw(key_of[3], (C, C * 4), (C * 4) ** -0.5, 0.375, ((1, 4),)),
        "cotangent": bell_draw(key_of[4], (COARSE, C, S * S), (COARSE * S * S) ** -0.5, 0.0234375, ((0, 8), (1, 4))),
        "edge_links": draw_edge_links(jax.random.fold_in(key_of[10], 71), 0),
        "edge_turns": plant(jax.random.randint(key_of[6], (TILES, 4), 0, 4), jax.random.fold_in(key_of[6], 1), 0, 3).astype(jnp.int32),
        "corner_links": draw_corner_links(jax.random.fold_in(key_of[10], 71), 0),
        "corner_turns": plant(jax.random.randint(key_of[8], (TILES, 4), 0, 4), jax.random.fold_in(key_of[8], 1), 0, 3).astype(jnp.int32),
        "child_slot": draw_child_slot(jax.random.fold_in(key_of[10], 71), 0),
    }


def edge_parts(tile_grid):
    side_len = tile_grid.shape[-1]
    edge_row = side_len - 1
    rim_strips = jnp.stack([tile_grid[:, :, 0, ::-1], tile_grid[:, :, :, 0], tile_grid[:, :, edge_row, :], tile_grid[:, :, ::-1, edge_row]], axis=1)
    corners = jnp.stack([tile_grid[:, :, 0, 0], tile_grid[:, :, edge_row, 0], tile_grid[:, :, edge_row, edge_row], tile_grid[:, :, 0, edge_row]], axis=1)
    return rim_strips, corners


def pad_tiles(tile_grid, every_rim, every_corner, edge_links, edge_turns, corner_links, corner_turns):
    side_index = jnp.arange(4, dtype=jnp.int32)[None, :]
    chosen = (side_index + 2 + edge_turns) % 4
    strips = every_rim[edge_links, chosen]
    corner_pick = (side_index + 2 + corner_turns) % 4
    corner_vals = every_corner[jnp.maximum(corner_links, 0), corner_pick]
    corner_vals = jnp.where((corner_links >= 0)[:, :, None], corner_vals, jnp.zeros_like(corner_vals))
    north_row = strips[:, 0]
    west_col = strips[:, 1, :, ::-1]
    south_row = strips[:, 2, :, ::-1]
    east_col = strips[:, 3]
    upper_row = jnp.concatenate([corner_vals[:, 0, :, None], north_row, corner_vals[:, 3, :, None]], axis=-1)
    bottom = jnp.concatenate([corner_vals[:, 1, :, None], south_row, corner_vals[:, 2, :, None]], axis=-1)
    middle = jnp.concatenate([west_col[:, :, :, None], tile_grid, east_col[:, :, :, None]], axis=-1)
    return jnp.concatenate([upper_row[:, :, None, :], middle, bottom[:, :, None, :]], axis=2)


def to_patches(tile_field):
    tile_count, channel_count, side_len = tile_field.shape[0], tile_field.shape[1], tile_field.shape[2]
    half_side = side_len // 2
    blocks = tile_field.reshape(tile_count, channel_count, half_side, 2, half_side, 2).transpose(0, 1, 3, 5, 2, 4)
    return blocks.reshape(tile_count, channel_count * 4, half_side * half_side)


def from_patches(patches, channel_count, side_len):
    tile_count = patches.shape[0]
    half_side = side_len // 2
    blocks = patches.reshape(tile_count, channel_count, 2, 2, half_side, half_side).transpose(0, 1, 4, 2, 5, 3)
    return blocks.reshape(tile_count, channel_count, side_len, side_len)


def join_quarters(by_slot, side_len):
    half_side = side_len // 2
    slot_count, channel_count = by_slot.shape[0], by_slot.shape[1]
    blocks = by_slot.reshape(slot_count // 4, 2, 2, channel_count, half_side, half_side).transpose(0, 3, 1, 4, 2, 5)
    return blocks.reshape(slot_count // 4, channel_count, side_len * side_len)


def split_coarse(coarse_field, side_len):
    half_side = side_len // 2
    tile_count, channel_count = coarse_field.shape[0], coarse_field.shape[1]
    blocks = coarse_field.reshape(tile_count, channel_count, 2, half_side, 2, half_side).transpose(0, 2, 4, 1, 3, 5)
    return blocks.reshape(tile_count * 4, channel_count, half_side * half_side)


def silu_slope(pre_act):
    squashed = jax.nn.sigmoid(pre_act)
    return squashed * (1.0 + pre_act * (1.0 - squashed))


def convolve(padded, kernel):
    filters = kernel.reshape(kernel.shape[0], -1, 3, 3)
    return lax.conv_general_dilated(padded, filters, (1, 1), "VALID", dimension_numbers=("NCHW", "OIHW", "NCHW"))


def reference(features, conv_weight, conv_bias, down_weight, cotangent, edge_links, edge_turns, corner_links, corner_turns, child_slot):
    tile_grid = features.reshape(TILES, C, S, S)
    rim_strips, corners = edge_parts(tile_grid)
    fine_cot = split_coarse(cotangent, S)[child_slot]
    kernel = conv_weight.astype(jnp.float32)
    down_float = down_weight.astype(jnp.float32)

    def block_step(totals, block_index):
        grad_conv, grad_bias, grad_down = totals
        first_tile = (block_index * TILE_DEV).astype(jnp.int32)
        tiles_here = lax.dynamic_slice_in_dim(tile_grid, first_tile, TILE_DEV, 0)
        links_here = lax.dynamic_slice_in_dim(edge_links, first_tile, TILE_DEV, 0)
        turns_here = lax.dynamic_slice_in_dim(edge_turns, first_tile, TILE_DEV, 0)
        clinks_here = lax.dynamic_slice_in_dim(corner_links, first_tile, TILE_DEV, 0)
        cturns_here = lax.dynamic_slice_in_dim(corner_turns, first_tile, TILE_DEV, 0)
        padded = pad_tiles(tiles_here, rim_strips, corners, links_here, turns_here, clinks_here, cturns_here).astype(jnp.float32)
        pre_act = convolve(padded, kernel) + conv_bias[None, :, None, None]
        hidden = jax.nn.silu(pre_act).astype(jnp.bfloat16)
        hidden = lax.optimization_barrier(hidden)
        patches = to_patches(hidden).astype(jnp.float32)
        quarter = jnp.einsum("ok,tkq->toq", down_float, patches).astype(jnp.bfloat16)
        cot_here = lax.dynamic_slice_in_dim(fine_cot, first_tile, TILE_DEV, 0).astype(jnp.float32)
        grad_down = grad_down + jnp.einsum("toq,tkq->ok", cot_here, patches)
        grad_hidden = from_patches(jnp.einsum("ok,toq->tkq", down_float, cot_here), C, S)
        grad_pre = (grad_hidden * silu_slope(pre_act)).astype(jnp.bfloat16)
        grad_pre = lax.optimization_barrier(grad_pre).astype(jnp.float32)
        grad_bias = grad_bias + jnp.sum(grad_pre, axis=(0, 2, 3))
        products = []
        for row_shift in range(3):
            for col_shift in range(3):
                window = padded[:, :, row_shift:row_shift + S, col_shift:col_shift + S]
                products.append(jnp.einsum("toyx,tiyx->oi", grad_pre, window))
        grad_conv = grad_conv + jnp.stack(products, axis=-1).reshape(C, C * 9)
        return (grad_conv, grad_bias, grad_down), quarter

    initial = (jnp.zeros((C, C * 9), jnp.float32), jnp.zeros((C,), jnp.float32), jnp.zeros((C, C * 4), jnp.float32))
    totals, quarters = lax.scan(block_step, initial, jnp.arange(N_TILE, dtype=jnp.int32))
    quarters = quarters.reshape(TILES, C, (S // 2) * (S // 2))
    ordered = jnp.zeros_like(quarters).at[child_slot].set(quarters)
    coarse = join_quarters(ordered, S)
    return (coarse, totals[0], totals[1], totals[2])
```

```python
import functools

import jax
import jax.numpy as jnp
import numpy as np
from jax import lax
from jax.experimental import pallas as pl
from jax.experimental.pallas import tpu as pltpu
from jax.sharding import PartitionSpec as P

C = 64
S = 64
H = S // 2
QUARTER = H * H
TAPS = 9
MESH = pl.DeviceIdType.MESH
F32 = jnp.float32
BF16 = jnp.bfloat16
VMEM_LIMIT = 50 * 1024 * 1024
PACK = 896


def rim_selector():
    pick = np.zeros((S * S, 4 * S), np.float32)
    for n in range(S):
        pick[S - 1 - n, n] = 1
        pick[n * S, S + n] = 1
        pick[(S - 1) * S + n, 2 * S + n] = 1
        pick[(S - 1 - n) * S + S - 1, 3 * S + n] = 1
    return pick


def phase_selector():
    lane = np.arange(8 * S)
    row, col = lane // S, lane % S
    target = ((row % 2) * 2 + col % 2) * 128 + (row // 2) * H + col // 2
    pick = np.zeros((8 * S, 8 * S), np.float32)
    pick[lane, target] = 1
    return pick


def half_selector():
    lane = np.arange(4 * S)
    row, col = lane // S, lane % S
    pick = np.zeros((4 * S, 4 * S), np.float32)
    pick[lane, (col // H) * 128 + row * H + col % H] = 1
    return pick


def side_selector():
    pick = np.zeros((2 * S, 4 * QUARTER), np.float32)
    for a in range(2):
        for u in range(H):
            pick[S - 1 - (2 * u + a), a * QUARTER + u * H] = 1
            pick[S + 2 * u + a, (2 + a) * QUARTER + u * H + H - 1] = 1
    return pick


def cap_selector():
    pick = np.zeros((4 * S, 8 * 128), np.float32)
    for wx in range(4):
        for v in range(H):
            x = 2 * v + wx - 1
            top = 128 + 0 if x < 0 else 128 + 3 if x >= S else x
            low = 128 + 1 if x < 0 else 128 + 2 if x >= S else S + S - 1 - x
            pick[top, wx * 128 + v] = 1
            pick[low, (4 + wx) * 128 + 96 + v] = 1
    return pick


def tap_selector():
    pick = np.zeros((C * TAPS, C * TAPS), np.float32)
    for i in range(C):
        for tap in range(TAPS):
            pick[i * TAPS + tap, tap * C + i] = 1
    return pick


def down_selector(n_chan):
    local = C // n_chan
    pick = np.zeros((n_chan, local * 4, C * 4), np.float32)
    for i in range(C):
        for ab in range(4):
            pick[i // local, (i % local) * 4 + ab, ab * C + i] = 1
    return pick


def dot(a, b):
    return jnp.dot(a, b, preferred_element_type=F32)


def dot_nt(a, b):
    return lax.dot_general(a, b, (((1,), (1,)), ((), ())), preferred_element_type=F32)


def greet(n_tile, n_chan, me_t, me_c):
    barrier = pltpu.get_barrier_semaphore()
    for k in range(1, n_tile):
        peer = lax.rem(me_t + k, n_tile)
        pl.semaphore_signal(barrier, inc=1, device_id=(peer, me_c), device_id_type=MESH)
    for k in range(1, n_chan):
        peer = lax.rem(me_c + k, n_chan)
        pl.semaphore_signal(barrier, inc=1, device_id=(me_t, peer), device_id_type=MESH)
    pl.semaphore_wait(barrier, n_tile - 1 + n_chan - 1)


def remote(src, dst, send_sem, recv_sem, device):
    copy = pltpu.make_async_remote_copy(
        src_ref=src,
        dst_ref=dst,
        send_sem=send_sem,
        recv_sem=recv_sem,
        device_id=device,
        device_id_type=MESH,
    )
    copy.start()
    return copy


def find_loop(table_ref, groups, tiles, wanted):
    def step(n, found):
        value = table_ref[n // tiles, n % tiles, 0]
        return tuple(jnp.where(value == w, n, f) for w, f in zip(wanted, found))

    return lax.fori_loop(0, groups * tiles, step, (jnp.int32(0),) * len(wanted))


def in_kernel(
    n_tile,
    n_chan,
    tiles,
    feat_ref,
    cot_ref,
    cw_ref,
    cb_ref,
    dw_ref,
    table_ref,
    el_ref,
    et_ref,
    cl_ref,
    ct_ref,
    rim_sel_ref,
    half_sel_ref,
    feat_out,
    halo_out,
    cot_out,
    cw_out,
    cb_out,
    dw_out,
    table_out,
    rims,
    halos,
    slots,
    cot_send,
    cot_recv,
    cot_group,
    table_smem,
    chan_send,
    chan_recv,
    tile_send,
    tile_recv,
    local_sem,
):
    me_t = lax.axis_index("tile")
    me_c = lax.axis_index("chan")
    per = tiles // n_chan
    local_chans = feat_ref.shape[1]

    greet(n_tile, n_chan, me_t, me_c)

    tile_copies = {}
    for k in range(1, n_tile):
        peer = (lax.rem(me_t + k, n_tile), me_c)
        tile_copies["table", k] = remote(
            table_ref, table_out.at[me_t], tile_send.at[0, k], tile_recv.at[0, k], peer
        )
    chan_copies = {}
    for k in range(1, n_chan):
        c = lax.rem(me_c + k, n_chan)
        peer = (me_t, c)
        chan_copies["feat", k] = remote(
            feat_ref.at[pl.ds(c * per, per)],
            feat_out.at[me_c],
            chan_send.at[0, k],
            chan_recv.at[0, k],
            peer,
        )
        chan_copies["cw", k] = remote(
            cw_ref, cw_out.at[me_c], chan_send.at[1, k], chan_recv.at[1, k], peer
        )
        chan_copies["cb", k] = remote(
            cb_ref, cb_out.at[me_c], chan_send.at[2, k], chan_recv.at[2, k], peer
        )
        chan_copies["dw", k] = remote(
            dw_ref, dw_out.at[me_c], chan_send.at[3, k], chan_recv.at[3, k], peer
        )

    pixels = feat_ref[...].reshape(tiles * local_chans, S * S)
    my_rims = dot(pixels, rim_sel_ref[...]).astype(BF16)
    rims[pl.ds(me_t, 1)] = my_rims.reshape(1, tiles, local_chans, 4 * S)
    for k in range(1, n_tile):
        peer = (lax.rem(me_t + k, n_tile), me_c)
        tile_copies["rims", k] = remote(
            rims.at[me_t], rims.at[me_t], tile_send.at[1, k], tile_recv.at[1, k], peer
        )

    coarse_tiles = cot_ref.shape[0]
    cots = cot_ref[...].reshape(coarse_tiles * local_chans, S * S)
    for j in range(16):
        moved = dot(cots[:, 256 * j : 256 * j + 256], half_sel_ref[...]).astype(BF16)
        lanes = slice((j % 8) * 128, (j % 8) * 128 + 128)
        for n in range(coarse_tiles):
            rows = moved[n * local_chans : (n + 1) * local_chans]
            slots[n * 4 + (j // 8) * 2, :, lanes] = rows[:, :128]
            slots[n * 4 + (j // 8) * 2 + 1, :, lanes] = rows[:, 128:]

    feat_out[pl.ds(me_c, 1)] = feat_ref[pl.ds(me_c * per, per)][None]
    cw_out[pl.ds(me_c, 1)] = cw_ref[...][None]
    cb_out[pl.ds(me_c, 1)] = cb_ref[...][None]
    dw_out[pl.ds(me_c, 1)] = dw_ref[...][None]
    table_out[pl.ds(me_t, 1)] = table_ref[...][None]

    for k in range(1, n_tile):
        tile_copies["table", k].wait()
    to_smem = pltpu.make_async_copy(table_out, table_smem, local_sem)
    to_smem.start()
    to_smem.wait()

    owners = find_loop(
        table_smem, n_tile, tiles, tuple(me_t * tiles + m for m in range(tiles))
    )
    homes = [f // tiles for f in owners]
    for d in range(n_tile):
        chosen = jnp.int32(0)
        for m in range(tiles):
            chosen = jnp.where(homes[m] == d, m, chosen)
        cot_send[d] = slots[chosen]
    for k in range(1, n_tile):
        d = lax.rem(me_t + k, n_tile)
        tile_copies["cot", k] = remote(
            cot_send.at[d],
            cot_recv.at[me_t],
            tile_send.at[2, k],
            tile_recv.at[2, k],
            (d, me_c),
        )
    cot_recv[pl.ds(me_t, 1)] = cot_send[pl.ds(me_t, 1)]

    for k in range(1, n_tile):
        tile_copies["rims", k].wait()
    lane = lax.broadcasted_iota(jnp.int32, (local_chans, 128), 1)
    for t in range(tiles):
        strips = []
        corners = jnp.zeros((local_chans, 128), F32)
        for k in range(4):
            link = el_ref[t, k]
            chosen = lax.rem(k + 2 + et_ref[t, k], 4)
            block = rims[link // tiles, lax.rem(link, tiles)].astype(F32)
            strip = block[:, :S]
            for r in range(1, 4):
                strip = jnp.where(chosen == r, block[:, r * S : r * S + S], strip)
            strips.append(strip)
            link = cl_ref[t, k]
            chosen = lax.rem(k + 3 + ct_ref[t, k], 4)
            held = jnp.maximum(link, 0)
            block = rims[held // tiles, lax.rem(held, tiles)].astype(F32)
            value = block[:, :1]
            for r in range(1, 4):
                value = jnp.where(chosen == r, block[:, r * S : r * S + 1], value)
            value = jnp.where(link >= 0, value, jnp.zeros_like(value))
            corners = jnp.where(lane == k, value, corners)
        north, west, south, east = strips
        halos[t] = jnp.concatenate([west, east, north, south, corners], axis=1).astype(BF16)
    for k in range(1, n_chan):
        c = lax.rem(me_c + k, n_chan)
        chan_copies["halo", k] = remote(
            halos.at[pl.ds(c * per, per)],
            halo_out.at[me_c],
            chan_send.at[4, k],
            chan_recv.at[4, k],
            (me_t, c),
        )
    halo_out[pl.ds(me_c, 1)] = halos[pl.ds(me_c * per, per)][None]

    for k in range(1, n_tile):
        tile_copies["cot", k].wait()
    for t in range(tiles):
        home = table_smem[me_t, t, 0] // tiles
        cot_group[t] = cot_recv[home]
    for k in range(1, n_chan):
        c = lax.rem(me_c + k, n_chan)
        chan_copies["cot", k] = remote(
            cot_group.at[pl.ds(c * per, per)],
            cot_out.at[me_c],
            chan_send.at[5, k],
            chan_recv.at[5, k],
            (me_t, c),
        )
    cot_out[pl.ds(me_c, 1)] = cot_group[pl.ds(me_c * per, per)][None]
    for copy in chan_copies.values():
        copy.wait()


def mid_kernel(
    n_chan,
    per,
    feat_ref,
    halo_ref,
    cot_ref,
    cw_ref,
    cb_ref,
    dw_ref,
    phase_sel_ref,
    side_sel_ref,
    cap_sel_ref,
    tap_sel_ref,
    down_sel_ref,
    quarter_ref,
    pack_ref,
    wide,
    window,
):
    taps = dot(cw_ref[...].reshape(C, C * TAPS), tap_sel_ref[...])
    none = jnp.zeros((C, C), F32)
    for a in range(2):
        for b in range(2):
            pieces = []
            for wy in range(4):
                for wx in range(4):
                    dy, dx = wy - a, wx - b
                    if 0 <= dy < 3 and 0 <= dx < 3:
                        tap = 3 * dy + dx
                        pieces.append(taps[:, tap * C : tap * C + C])
                    else:
                        pieces.append(none)
            row = (a * 2 + b) * C
            wide[row : row + C, :] = jnp.concatenate(pieces, axis=1).astype(BF16)
    down = dot(dw_ref[0], down_sel_ref[0])
    for c in range(1, n_chan):
        down = down + dot(dw_ref[c], down_sel_ref[c])
    down_t = down.T.astype(BF16)
    down = down.astype(BF16)
    bias = cb_ref[...].reshape(C, 128)[:, :1]
    bias = jnp.concatenate([bias] * 4, axis=0)

    lane = lax.broadcasted_iota(jnp.int32, (C, QUARTER), 1)
    first_col = lax.rem(lane, H) == 0
    last_col = lax.rem(lane, H) == H - 1
    lane_cap = lax.broadcasted_iota(jnp.int32, (C, 128), 1)

    grad_wide = None
    grad_down = None
    grad_bias = None
    for t in range(per):
        halo = halo_ref[:, t].reshape(C, 6 * S)
        sides = dot(halo[:, : 2 * S], side_sel_ref[...])
        caps = dot(halo[:, 2 * S :], cap_sel_ref[...])
        pixels = feat_ref[:, t].reshape(C, S * S)
        chunks = [
            dot(pixels[:, 512 * j : 512 * j + 512], phase_sel_ref[...]) for j in range(8)
        ]
        phase = [
            jnp.concatenate([chunk[:, p * 128 : p * 128 + 128] for chunk in chunks], axis=1)
            for p in range(4)
        ]
        for a in range(2):
            even, odd = phase[a * 2], phase[a * 2 + 1]
            west = jnp.where(
                first_col, sides[:, a * QUARTER : (a + 1) * QUARTER], pltpu.roll(odd, 1, 1)
            )
            east = jnp.where(
                last_col,
                sides[:, (2 + a) * QUARTER : (3 + a) * QUARTER],
                pltpu.roll(even, QUARTER - 1, 1),
            )
            for wx, middle in enumerate((west, even, odd, east)):
                row = ((1 + a) * 4 + wx) * C
                window[row : row + C, :] = middle.astype(BF16)
                if a == 1:
                    moved = pltpu.roll(middle, H, 1)
                    cap = caps[:, wx * 128 : wx * 128 + 128]
                    head = jnp.where(lane_cap < H, cap, moved[:, :128])
                    moved = jnp.concatenate([head, moved[:, 128:]], axis=1)
                    row = wx * C
                else:
                    moved = pltpu.roll(middle, QUARTER - H, 1)
                    cap = caps[:, (4 + wx) * 128 : (5 + wx) * 128]
                    tail = jnp.where(lane_cap >= 128 - H, cap, moved[:, QUARTER - 128 :])
                    moved = jnp.concatenate([moved[:, : QUARTER - 128], tail], axis=1)
                    row = (12 + wx) * C
                window[row : row + C, :] = moved.astype(BF16)
        pre = dot(wide[...], window[...]) + bias
        squashed = 1.0 / (1.0 + jnp.exp(-pre))
        hidden = (pre * squashed).astype(BF16)
        quarter_ref[t] = dot(down, hidden).astype(BF16)
        back = cot_ref[:, t].reshape(C, QUARTER)
        grad_hidden = dot(down_t, back)
        grad_pre = (grad_hidden * (squashed * (1.0 + pre * (1.0 - squashed)))).astype(BF16)
        part_down = dot_nt(hidden, back)
        part_bias = jnp.sum(grad_pre.astype(F32), axis=1, keepdims=True)
        part_wide = dot_nt(grad_pre, window[...])
        if t == 0:
            grad_down, grad_bias, grad_wide = part_down, part_bias, part_wide
        else:
            grad_down = grad_down + part_down
            grad_bias = grad_bias + part_bias
            grad_wide = grad_wide + part_wide
    for dy in range(3):
        for dx in range(3):
            total = None
            for a in range(2):
                for b in range(2):
                    row = (a * 2 + b) * C
                    col = ((a + dy) * 4 + b + dx) * C
                    piece = grad_wide[row : row + C, col : col + C]
                    total = piece if total is None else total + piece
            tap = 3 * dy + dx
            pack_ref[:, tap * C : tap * C + C] = total
    bias_sum = grad_bias[:C] + grad_bias[C : 2 * C] + grad_bias[2 * C : 3 * C] + grad_bias[3 * C :]
    pack_ref[:, TAPS * C : TAPS * C + C] = jnp.broadcast_to(bias_sum, (C, C))
    for ab in range(4):
        col = (TAPS + 1 + ab) * C
        pack_ref[:, col : col + C] = grad_down[ab * C : ab * C + C]


def out_kernel(
    n_tile,
    n_chan,
    tiles,
    quarter_ref,
    pack_ref,
    table_ref,
    join_sel_ref,
    coarse_out,
    grads_out,
    group,
    quarter_send,
    quarter_recv,
    pack_recv,
    pack_all,
    chan_send,
    chan_recv,
    tile_send,
    tile_recv,
):
    me_t = lax.axis_index("tile")
    me_c = lax.axis_index("chan")
    local_chans = coarse_out.shape[1]

    greet(n_tile, n_chan, me_t, me_c)

    chan_copies = {}
    for k in range(1, n_chan):
        c = lax.rem(me_c + k, n_chan)
        chan_rows = pl.ds(pl.multiple_of(c * local_chans, local_chans), local_chans)
        chan_copies["quarter", k] = remote(
            quarter_ref.at[:, chan_rows],
            group.at[me_c],
            chan_send.at[0, k],
            chan_recv.at[0, k],
            (me_t, c),
        )
    for k in range(1, n_chan):
        c = lax.rem(me_c + k, n_chan)
        chan_rows = pl.ds(pl.multiple_of(c * local_chans, local_chans), local_chans)
        chan_copies["pack", k] = remote(
            pack_ref.at[chan_rows],
            pack_recv.at[me_c],
            chan_send.at[1, k],
            chan_recv.at[1, k],
            (me_t, c),
        )
    my_rows = pl.ds(pl.multiple_of(me_c * local_chans, local_chans), local_chans)
    group[pl.ds(me_c, 1)] = quarter_ref[:, my_rows][None]
    pack_recv[pl.ds(me_c, 1)] = pack_ref[my_rows][None]

    homes = [table_ref[me_t, t, 0] // tiles for t in range(tiles)]
    sources = find_loop(
        table_ref, n_tile, tiles, tuple(me_t * tiles + m for m in range(tiles))
    )
    per = group.shape[1]

    for k in range(1, n_chan):
        chan_copies["quarter", k].wait()
    for d in range(n_tile):
        chosen = jnp.int32(0)
        for t in range(tiles):
            chosen = jnp.where(homes[t] == d, t, chosen)
        quarter_send[d] = group[chosen // per, lax.rem(chosen, per)]
    tile_copies = {}
    for k in range(1, n_tile):
        d = lax.rem(me_t + k, n_tile)
        tile_copies["quarter", k] = remote(
            quarter_send.at[d],
            quarter_recv.at[me_t],
            tile_send.at[0, k],
            tile_recv.at[0, k],
            (d, me_c),
        )
    quarter_recv[pl.ds(me_t, 1)] = quarter_send[pl.ds(me_t, 1)]

    for k in range(1, n_chan):
        chan_copies["pack", k].wait()
    total = pack_recv[0]
    for c in range(1, n_chan):
        total = total + pack_recv[c]
    pack_all[pl.ds(me_t, 1)] = total[None]
    for k in range(1, n_tile):
        d = lax.rem(me_t + k, n_tile)
        tile_copies["pack", k] = remote(
            pack_all.at[me_t],
            pack_all.at[me_t],
            tile_send.at[1, k],
            tile_recv.at[1, k],
            (d, me_c),
        )

    for k in range(1, n_tile):
        tile_copies["quarter", k].wait()
    placed = [quarter_recv[f // tiles] for f in sources]
    for n in range(coarse_out.shape[0]):
        for j in range(16):
            lanes = slice((j % 8) * 128, (j % 8) * 128 + 128)
            q = n * 4 + (j // 8) * 2
            both = jnp.concatenate([placed[q][:, lanes], placed[q + 1][:, lanes]], axis=1)
            coarse_out[n, :, 256 * j : 256 * j + 256] = dot(both, join_sel_ref[...]).astype(BF16)

    for k in range(1, n_tile):
        tile_copies["pack", k].wait()
    total = pack_all[0]
    for s in range(1, n_tile):
        total = total + pack_all[s]
    grads_out[...] = total


def on_device(
    n_tile,
    n_chan,
    features,
    conv_weight,
    conv_bias,
    down_weight,
    cotangent,
    edge_links,
    edge_turns,
    corner_links,
    corner_turns,
    child_slot,
):
    tiles, local = features.shape[0], features.shape[1]
    per = tiles // n_chan
    vmem = pl.BlockSpec(memory_space=pltpu.VMEM)
    smem = pl.BlockSpec(memory_space=pltpu.SMEM)
    table = jnp.broadcast_to(child_slot[:, None], (tiles, 128))
    bias = jnp.broadcast_to(conv_bias[:, None], (local, 128))

    def const(values):
        return jnp.asarray(values, BF16)

    half = half_selector()
    shapes = [
        jax.ShapeDtypeStruct((n_chan, per, local, S * S), BF16),
        jax.ShapeDtypeStruct((n_chan, per, local, 6 * S), BF16),
        jax.ShapeDtypeStruct((n_chan, per, local, QUARTER), BF16),
        jax.ShapeDtypeStruct((n_chan, local, C * TAPS), BF16),
        jax.ShapeDtypeStruct((n_chan, local, 128), F32),
        jax.ShapeDtypeStruct((n_chan, C, local * 4), BF16),
        jax.ShapeDtypeStruct((n_tile, tiles, 128), jnp.int32),
    ]
    feat_t, halo_t, cot_t, cw_t, cb_t, dw_t, table_all = pl.pallas_call(
        functools.partial(in_kernel, n_tile, n_chan, tiles),
        out_shape=shapes,
        in_specs=[vmem] * 6 + [smem] * 4 + [vmem] * 2,
        out_specs=[vmem] * len(shapes),
        scratch_shapes=[
            pltpu.VMEM((n_tile, tiles, local, 4 * S), BF16),
            pltpu.VMEM((tiles, local, 6 * S), BF16),
            pltpu.VMEM((tiles, local, QUARTER), BF16),
            pltpu.VMEM((n_tile, local, QUARTER), BF16),
            pltpu.VMEM((n_tile, local, QUARTER), BF16),
            pltpu.VMEM((tiles, local, QUARTER), BF16),
            pltpu.SMEM((n_tile, tiles, 128), jnp.int32),
            pltpu.SemaphoreType.DMA((6, n_chan)),
            pltpu.SemaphoreType.DMA((6, n_chan)),
            pltpu.SemaphoreType.DMA((3, n_tile)),
            pltpu.SemaphoreType.DMA((3, n_tile)),
            pltpu.SemaphoreType.DMA,
        ],
        compiler_params=pltpu.CompilerParams(
            collective_id=0, has_side_effects=True, vmem_limit_bytes=VMEM_LIMIT
        ),
        name="exchange_inputs",
    )(
        features,
        cotangent,
        conv_weight,
        bias,
        down_weight,
        table,
        edge_links,
        edge_turns,
        corner_links,
        corner_turns,
        const(rim_selector()),
        const(half),
    )
    quarter, pack = pl.pallas_call(
        functools.partial(mid_kernel, n_chan, per),
        out_shape=[
            jax.ShapeDtypeStruct((per, C, QUARTER), BF16),
            jax.ShapeDtypeStruct((C, PACK), F32),
        ],
        in_specs=[vmem] * 11,
        out_specs=[vmem] * 2,
        scratch_shapes=[
            pltpu.VMEM((4 * C, 16 * C), BF16),
            pltpu.VMEM((16 * C, QUARTER), BF16),
        ],
        compiler_params=pltpu.CompilerParams(vmem_limit_bytes=VMEM_LIMIT),
        name="convolve",
    )(
        feat_t,
        halo_t,
        cot_t,
        cw_t,
        cb_t,
        dw_t,
        const(phase_selector()),
        const(side_selector()),
        const(cap_selector()),
        const(tap_selector()),
        const(down_selector(n_chan)),
    )
    coarse, grads = pl.pallas_call(
        functools.partial(out_kernel, n_tile, n_chan, tiles),
        out_shape=[
            jax.ShapeDtypeStruct(cotangent.shape, BF16),
            jax.ShapeDtypeStruct((local, PACK), F32),
        ],
        in_specs=[vmem, vmem, smem, vmem],
        out_specs=[vmem] * 2,
        scratch_shapes=[
            pltpu.VMEM((n_chan, per, local, QUARTER), BF16),
            pltpu.VMEM((n_tile, local, QUARTER), BF16),
            pltpu.VMEM((n_tile, local, QUARTER), BF16),
            pltpu.VMEM((n_chan, local, PACK), F32),
            pltpu.VMEM((n_tile, local, PACK), F32),
            pltpu.SemaphoreType.DMA((2, n_chan)),
            pltpu.SemaphoreType.DMA((2, n_chan)),
            pltpu.SemaphoreType.DMA((2, n_tile)),
            pltpu.SemaphoreType.DMA((2, n_tile)),
        ],
        compiler_params=pltpu.CompilerParams(
            collective_id=1, has_side_effects=True, vmem_limit_bytes=VMEM_LIMIT
        ),
        name="exchange_outputs",
    )(quarter, pack, table_all, const(half.T))
    grad_conv = grads[:, : C * TAPS].reshape(local, TAPS, C)
    grad_conv = grad_conv.transpose(0, 2, 1).reshape(local, C * TAPS)
    grad_bias = grads[:, C * TAPS]
    grad_down = grads[:, C * (TAPS + 1) :].reshape(local, 4, C)
    grad_down = grad_down.transpose(2, 0, 1).reshape(C, local * 4)
    return (coarse, grad_conv, grad_bias, grad_down)


def solution(mesh):
    n_tile, n_chan = mesh.shape["tile"], mesh.shape["chan"]
    in_specs = (
        P("tile", "chan", None),
        P("chan", None),
        P("chan"),
        P(None, "chan"),
        P("tile", "chan", None),
        P("tile", None),
        P("tile", None),
        P("tile", None),
        P("tile", None),
        P("tile"),
    )
    out_specs = (P("tile", "chan", None), P("chan", None), P("chan"), P(None, "chan"))
    return jax.shard_map(
        functools.partial(on_device, n_tile, n_chan),
        mesh=mesh,
        in_specs=in_specs,
        out_specs=out_specs,
        check_vma=False,
    )
```

```python
import functools

import jax
import jax.numpy as jnp
import numpy as np
from jax import lax
from jax.experimental import pallas as pl
from jax.experimental.pallas import tpu as pltpu
from jax.sharding import PartitionSpec as P

C = 64
S = 64
H = S // 2
QUARTER = H * H
TAPS = 9
MESH = pl.DeviceIdType.MESH
F32 = jnp.float32
BF16 = jnp.bfloat16
VMEM_LIMIT = 50 * 1024 * 1024
PACK = 1024
BIAS_COL = TAPS * C
DOWN_COL = BIAS_COL + C
SLOT_LANE = 16


def rim_selector():
    pick = np.zeros((S * S, 4 * S), np.float32)
    for n in range(S):
        pick[S - 1 - n, n] = 1
        pick[n * S, S + n] = 1
        pick[(S - 1) * S + n, 2 * S + n] = 1
        pick[(S - 1 - n) * S + S - 1, 3 * S + n] = 1
    return pick


def phase_selector():
    lane = np.arange(8 * S)
    row, col = lane // S, lane % S
    target = ((row % 2) * 2 + col % 2) * 128 + (row // 2) * H + col // 2
    pick = np.zeros((8 * S, 8 * S), np.float32)
    pick[lane, target] = 1
    return pick


def half_selector():
    lane = np.arange(4 * S)
    row, col = lane // S, lane % S
    pick = np.zeros((4 * S, 4 * S), np.float32)
    pick[lane, (col // H) * 128 + row * H + col % H] = 1
    return pick


def side_selector():
    pick = np.zeros((2 * S, 4 * QUARTER), np.float32)
    for a in range(2):
        for u in range(H):
            pick[S - 1 - (2 * u + a), a * QUARTER + u * H] = 1
            pick[S + 2 * u + a, (2 + a) * QUARTER + u * H + H - 1] = 1
    return pick


def cap_selector():
    pick = np.zeros((4 * S, 8 * 128), np.float32)
    for wx in range(4):
        for v in range(H):
            x = 2 * v + wx - 1
            top = 128 + 0 if x < 0 else 128 + 3 if x >= S else x
            low = 128 + 1 if x < 0 else 128 + 2 if x >= S else S + S - 1 - x
            pick[top, wx * 128 + v] = 1
            pick[low, (4 + wx) * 128 + 96 + v] = 1
    return pick


def tap_selector():
    pick = np.zeros((C * TAPS, C * TAPS), np.float32)
    for i in range(C):
        for tap in range(TAPS):
            pick[i * TAPS + tap, tap * C + i] = 1
    return pick


def down_selector(n_chan):
    local = C // n_chan
    pick = np.zeros((n_chan, local * 4, C * 4), np.float32)
    for i in range(C):
        for ab in range(4):
            pick[i // local, (i % local) * 4 + ab, ab * C + i] = 1
    return pick


def dot(a, b):
    return jnp.dot(a, b, preferred_element_type=F32)


def dot_nt(a, b):
    return lax.dot_general(a, b, (((1,), (1,)), ((), ())), preferred_element_type=F32)


def split_dot_nt(a, selector):
    high = a.astype(BF16)
    rest = a - high.astype(F32)
    middle = rest.astype(BF16)
    low = (rest - middle.astype(F32)).astype(BF16)
    return dot_nt(high, selector) + dot_nt(middle, selector) + dot_nt(low, selector)


def greet(n_tile, n_chan, me_t, me_c):
    barrier = pltpu.get_barrier_semaphore()
    for k in range(1, n_tile):
        peer = lax.rem(me_t + k, n_tile)
        pl.semaphore_signal(barrier, inc=1, device_id=(peer, me_c), device_id_type=MESH)
    for k in range(1, n_chan):
        peer = lax.rem(me_c + k, n_chan)
        pl.semaphore_signal(barrier, inc=1, device_id=(me_t, peer), device_id_type=MESH)


def remote(src, dst, send_sem, recv_sem, device):
    copy = pltpu.make_async_remote_copy(
        src_ref=src,
        dst_ref=dst,
        send_sem=send_sem,
        recv_sem=recv_sem,
        device_id=device,
        device_id_type=MESH,
    )
    copy.start()
    return copy


def find_owners(table, groups, tiles, wanted):
    def step(s, found):
        for t in range(tiles):
            value = table[s, t, SLOT_LANE]
            found = tuple(jnp.where(value == w, s, f) for w, f in zip(wanted, found))
        return found

    return lax.fori_loop(0, groups, step, (jnp.int32(0),) * len(wanted))


def widen_weights(taps, wide):
    none = jnp.zeros((C, C), F32)
    for a in range(2):
        for b in range(2):
            pieces = []
            for wy in range(4):
                for wx in range(4):
                    dy, dx = wy - a, wx - b
                    if 0 <= dy < 3 and 0 <= dx < 3:
                        tap = 3 * dy + dx
                        pieces.append(taps[:, tap * C : tap * C + C])
                    else:
                        pieces.append(none)
            row = (a * 2 + b) * C
            wide[row : row + C, :] = jnp.concatenate(pieces, axis=1).astype(BF16)


def fill_window(phase, sides, caps, window, t):
    lane = lax.broadcasted_iota(jnp.int32, (C, QUARTER), 1)
    first_col = lax.rem(lane, H) == 0
    last_col = lax.rem(lane, H) == H - 1
    lane_cap = lax.broadcasted_iota(jnp.int32, (C, 128), 1)
    for a in range(2):
        even, odd = phase[a * 2], phase[a * 2 + 1]
        west = jnp.where(
            first_col, sides[:, a * QUARTER : (a + 1) * QUARTER], pltpu.roll(odd, 1, 1)
        )
        east = jnp.where(
            last_col,
            sides[:, (2 + a) * QUARTER : (3 + a) * QUARTER],
            pltpu.roll(even, QUARTER - 1, 1),
        )
        for wx, middle in enumerate((west, even, odd, east)):
            row = ((1 + a) * 4 + wx) * C
            window[t, row : row + C, :] = middle.astype(BF16)
            if a == 1:
                moved = pltpu.roll(middle, H, 1)
                cap = caps[:, wx * 128 : wx * 128 + 128]
                head = jnp.where(lane_cap < H, cap, moved[:, :128])
                moved = jnp.concatenate([head, moved[:, 128:]], axis=1)
                row = wx * C
            else:
                moved = pltpu.roll(middle, QUARTER - H, 1)
                cap = caps[:, (4 + wx) * 128 : (5 + wx) * 128]
                tail = jnp.where(lane_cap >= 128 - H, cap, moved[:, QUARTER - 128 :])
                moved = jnp.concatenate([moved[:, : QUARTER - 128], tail], axis=1)
                row = (12 + wx) * C
            window[t, row : row + C, :] = moved.astype(BF16)


def level_kernel(
    n_tile,
    n_chan,
    tiles,
    feat_hbm,
    cot_hbm,
    cw_hbm,
    dw_hbm,
    table_hbm,
    rim_sel_hbm,
    half_sel_hbm,
    phase_sel_hbm,
    side_sel_hbm,
    cap_sel_hbm,
    tap_sel_hbm,
    down_sel_hbm,
    cb_smem,
    placed_out,
    grads_out,
    feat,
    cot,
    rim_sel,
    half_sel,
    phase_sel,
    side_sel,
    cap_sel,
    tap_sel,
    down_sel,
    feat_all,
    cw_all,
    dw_all,
    cb_all,
    table_all,
    table,
    rims,
    halos,
    halo_all,
    slots,
    cot_send,
    cot_recv,
    cot_group,
    cot_all,
    wide,
    phases,
    window,
    pre_act,
    hidden,
    quarter,
    quarter_group,
    quarter_send,
    quarter_recv,
    pack,
    pack_recv,
    pieces,
    pieces_recv,
    local_sem,
    chan_send,
    chan_recv,
    tile_send,
    tile_recv,
    rim_send,
    rim_recv,
):
    me_t = lax.axis_index("tile")
    me_c = lax.axis_index("chan")
    per = tiles // n_chan
    local = feat.shape[1]
    n_outer = n_tile // 2
    outer, inner = me_t // 2, lax.rem(me_t, 2)

    greet(n_tile, n_chan, me_t, me_c)

    def fetch(src, dst, k):
        copy = pltpu.make_async_copy(src, dst, local_sem.at[k])
        copy.start()
        return copy

    get_feat = fetch(feat_hbm, feat, 0)
    get_rim_sel = fetch(rim_sel_hbm, rim_sel, 1)
    get_cot = fetch(cot_hbm, cot, 2)
    get_half_sel = fetch(half_sel_hbm, half_sel, 3)
    get_table = fetch(table_hbm, table_all.at[me_t], 4)
    get_own = [
        fetch(cw_hbm, cw_all.at[me_c], 5),
        fetch(dw_hbm, dw_all.at[me_c], 6),
        fetch(feat_hbm.at[pl.ds(me_c * per, per)], feat_all.at[me_c], 7),
        fetch(phase_sel_hbm, phase_sel, 8),
        fetch(side_sel_hbm, side_sel, 9),
        fetch(cap_sel_hbm, cap_sel, 10),
        fetch(tap_sel_hbm, tap_sel, 11),
        fetch(down_sel_hbm, down_sel, 12),
    ]
    row = lax.broadcasted_iota(jnp.int32, (local, 128), 0)
    bias = jnp.zeros((local, 128), F32)
    for n in range(local):
        bias = jnp.where(row == n, cb_smem[n], bias)
    cb_all[pl.ds(me_c, 1)] = bias[None]

    get_feat.wait()
    get_rim_sel.wait()
    pixels = feat[...].reshape(tiles * local, S * S)
    my_rims = dot(pixels, rim_sel[...]).astype(BF16)
    rims[pl.ds(me_t, 1)] = my_rims.reshape(1, tiles, local, 4 * S)
    get_table.wait()

    pl.semaphore_wait(pltpu.get_barrier_semaphore(), n_tile - 1 + n_chan - 1)

    def to_tiles(kind, src, dst):
        copies = []
        for k in range(1, n_tile):
            d = lax.rem(me_t + k, n_tile)
            copies.append(
                remote(
                    src(d), dst, tile_send.at[kind, k], tile_recv.at[kind, k], (d, me_c)
                )
            )
        return copies

    def to_chans(kind, src, dst):
        copies = []
        for k in range(1, n_chan):
            c = lax.rem(me_c + k, n_chan)
            copies.append(
                remote(
                    src(c), dst, chan_send.at[kind, k], chan_recv.at[kind, k], (me_t, c)
                )
            )
        return copies

    def finish(copies):
        for copy in copies:
            copy.wait()

    def chan_rows(c):
        return pl.ds(pl.multiple_of(c * local, local), local)

    table_copies = to_tiles(0, lambda d: table_all.at[me_t], table_all.at[me_t])
    across = outer * 2 + 1 - inner
    forwards = [
        remote(
            rims.at[me_t], rims.at[me_t], rim_send.at[1, 0], rim_recv.at[1, 0], (across, me_c)
        )
    ]
    straight = []
    for k in range(1, n_outer):
        d = lax.rem(outer + k, n_outer) * 2 + inner
        straight.append(
            remote(rims.at[me_t], rims.at[me_t], rim_send.at[0, k], rim_recv.at[0, k], (d, me_c))
        )
    small_copies = (
        to_chans(1, lambda c: cw_hbm, cw_all.at[me_c])
        + to_chans(2, lambda c: dw_hbm, dw_all.at[me_c])
        + to_chans(3, lambda c: cb_all.at[me_c], cb_all.at[me_c])
    )
    feat_copies = to_chans(0, lambda c: feat_hbm.at[pl.ds(c * per, per)], feat_all.at[me_c])

    get_cot.wait()
    get_half_sel.wait()
    coarse_tiles = cot.shape[0]
    cots = cot[...].reshape(coarse_tiles * local, S * S)
    for j in range(16):
        moved = dot(cots[:, 256 * j : 256 * j + 256], half_sel[...]).astype(BF16)
        lanes = slice((j % 8) * 128, (j % 8) * 128 + 128)
        for n in range(coarse_tiles):
            rows = moved[n * local : (n + 1) * local]
            slots[n * 4 + (j // 8) * 2, :, lanes] = rows[:, :128]
            slots[n * 4 + (j // 8) * 2 + 1, :, lanes] = rows[:, 128:]

    finish(table_copies)
    to_smem = pltpu.make_async_copy(table_all, table, local_sem.at[13])
    to_smem.start()
    to_smem.wait()
    homes = find_owners(table, n_tile, tiles, tuple(me_t * tiles + m for m in range(tiles)))
    owners = [table[me_t, t, SLOT_LANE] // tiles for t in range(tiles)]
    for d in range(n_tile):
        chosen = jnp.int32(0)
        for m in range(tiles):
            chosen = jnp.where(homes[m] == d, m, chosen)
        cot_send[d] = slots[chosen]
    cot_recv[pl.ds(me_t, 1)] = cot_send[pl.ds(me_t, 1)]

    for k in range(1, n_outer):
        straight[k - 1].wait_recv()
        source = lax.rem(outer + n_outer - k, n_outer) * 2 + inner
        forwards.append(
            remote(
                rims.at[source],
                rims.at[source],
                rim_send.at[1, k],
                rim_recv.at[1, k],
                (across, me_c),
            )
        )
    cot_copies = to_tiles(1, lambda d: cot_send.at[d], cot_recv.at[me_t])

    finish(get_own)
    finish(small_copies)
    widen_weights(dot(cw_all[...].reshape(C, C * TAPS), tap_sel[...]), wide)
    down = jnp.zeros((C, 4 * C), F32)
    for c in range(n_chan):
        down = down + dot(dw_all[c], down_sel[c])
    down_t = down.T.astype(BF16)
    down = down.astype(BF16)

    finish(forwards)
    for copy in straight:
        copy.wait_send()
    lane = lax.broadcasted_iota(jnp.int32, (local, 128), 1)
    for t in range(tiles):
        strips = []
        corners = jnp.zeros((local, 128), F32)
        for k in range(4):
            link = table[me_t, t, k]
            chosen = lax.rem(k + 2 + table[me_t, t, 4 + k], 4)
            block = rims[link // tiles, lax.rem(link, tiles)].astype(F32)
            strip = block[:, :S]
            for r in range(1, 4):
                strip = jnp.where(chosen == r, block[:, r * S : r * S + S], strip)
            strips.append(strip)
            link = table[me_t, t, 8 + k]
            chosen = lax.rem(k + 3 + table[me_t, t, 12 + k], 4)
            held = jnp.maximum(link, 0)
            block = rims[held // tiles, lax.rem(held, tiles)].astype(F32)
            value = block[:, :1]
            for r in range(1, 4):
                value = jnp.where(chosen == r, block[:, r * S : r * S + 1], value)
            value = jnp.where(link >= 0, value, jnp.zeros_like(value))
            corners = jnp.where(lane == k, value, corners)
        north, west, south, east = strips
        halos[t] = jnp.concatenate([west, east, north, south, corners], axis=1).astype(BF16)
    halo_all[pl.ds(me_c, 1)] = halos[pl.ds(me_c * per, per)][None]
    halo_copies = to_chans(4, lambda c: halos.at[pl.ds(c * per, per)], halo_all.at[me_c])

    finish(feat_copies)
    for t in range(per):
        pixels = feat_all[:, t].reshape(C, S * S)
        for j in range(8):
            moved = dot(pixels[:, 512 * j : 512 * j + 512], phase_sel[...])
            for p in range(4):
                phases[t, p, :, 128 * j : 128 * j + 128] = moved[:, p * 128 : p * 128 + 128]

    finish(halo_copies)
    bias = jnp.concatenate([cb_all[...].reshape(C, 128)[:, :1]] * 4, axis=0)
    for t in range(per):
        halo = halo_all[:, t].reshape(C, 6 * S)
        sides = dot(halo[:, : 2 * S], side_sel[...])
        caps = dot(halo[:, 2 * S :], cap_sel[...])
        fill_window([phases[t, p] for p in range(4)], sides, caps, window, t)
        pre = dot(wide[...], window[t]) + bias
        pre_act[t] = pre
        hidden[t] = (pre * (1.0 / (1.0 + jnp.exp(-pre)))).astype(BF16)
        quarter[t] = dot(down, hidden[t]).astype(BF16)
    quarter_group[pl.ds(me_c, 1)] = quarter[:, chan_rows(me_c)][None]
    quarter_copies = to_chans(
        5, lambda c: quarter.at[:, chan_rows(c)], quarter_group.at[me_c]
    )

    finish(cot_copies)
    for t in range(tiles):
        cot_group[t] = cot_recv[owners[t]]
    cot_all[pl.ds(me_c, 1)] = cot_group[pl.ds(me_c * per, per)][None]
    cot_chan_copies = to_chans(
        6, lambda c: cot_group.at[pl.ds(c * per, per)], cot_all.at[me_c]
    )

    finish(quarter_copies)
    for d in range(n_tile):
        chosen = jnp.int32(0)
        for t in range(tiles):
            chosen = jnp.where(owners[t] == d, t, chosen)
        quarter_send[d] = quarter_group[chosen // per, lax.rem(chosen, per)]
    quarter_recv[pl.ds(me_t, 1)] = quarter_send[pl.ds(me_t, 1)]
    quarter_copies = to_tiles(2, lambda d: quarter_send.at[d], quarter_recv.at[me_t])

    finish(cot_chan_copies)
    grad_wide = jnp.zeros((4 * C, 16 * C), F32)
    grad_down = jnp.zeros((C, 4 * C), F32)
    grad_bias = jnp.zeros((8, 4 * C), F32)
    ones = jnp.ones((8, QUARTER), BF16)
    for t in range(per):
        back = cot_all[:, t].reshape(C, QUARTER)
        pre = pre_act[t]
        squashed = 1.0 / (1.0 + jnp.exp(-pre))
        slope = squashed * (1.0 + pre * (1.0 - squashed))
        grad_pre = (dot(down_t, back) * slope).astype(BF16)
        grad_down = grad_down + dot_nt(back, hidden[t])
        grad_bias = grad_bias + dot_nt(ones, grad_pre)
        grad_wide = grad_wide + dot_nt(grad_pre, window[t])
    taps = []
    for dy in range(3):
        for dx in range(3):
            total = jnp.zeros((C, C), F32)
            for a in range(2):
                for b in range(2):
                    row = (a * 2 + b) * C
                    col = ((a + dy) * 4 + b + dx) * C
                    total = total + grad_wide[row : row + C, col : col + C]
            taps.append(total)
    pack[:, : TAPS * C] = split_dot_nt(jnp.concatenate(taps, axis=1), tap_sel[...])
    pack[:, TAPS * C :] = jnp.zeros((C, PACK - TAPS * C), F32)
    grad_down = split_dot_nt(grad_down, down_sel[...].reshape(4 * C, 4 * C))
    total = grad_bias[:1, :C]
    for ab in range(1, 4):
        total = total + grad_bias[:1, ab * C : ab * C + C]
    for c in range(n_chan):
        rows = slice(c * local, c * local + local)
        pack[c * local : c * local + 1, BIAS_COL : BIAS_COL + local] = total[:, rows]
        wide_cols = slice(c * 4 * local, (c + 1) * 4 * local)
        for n in range(C // local):
            col = DOWN_COL + n * 4 * local
            pack[rows, col : col + 4 * local] = grad_down[n * local : (n + 1) * local, wide_cols]

    pack_recv[pl.ds(me_c, 1)] = pack[chan_rows(me_c)][None]
    finish(to_chans(7, lambda c: pack.at[chan_rows(c)], pack_recv.at[me_c]))
    total = pack_recv[0]
    for c in range(1, n_chan):
        total = total + pack_recv[c]
    n_pieces = PACK // 128
    if n_tile == n_pieces:
        for n in range(n_pieces):
            pieces[n] = total[:, n * 128 : n * 128 + 128]
        pieces_recv[pl.ds(me_t, 1)] = pieces[pl.ds(me_t, 1)]
        finish(to_tiles(3, lambda d: pieces.at[d], pieces_recv.at[me_t]))
        total = pieces_recv[0]
        for s in range(1, n_tile):
            total = total + pieces_recv[s]
        grads_out[pl.ds(me_t, 1)] = total[None]
        finish(to_tiles(4, lambda d: grads_out.at[me_t], grads_out.at[me_t]))
    else:
        pieces[pl.ds(me_t, 1)] = total[None]
        finish(to_tiles(3, lambda d: pieces.at[me_t], pieces.at[me_t]))
        total = pieces[0]
        for s in range(1, n_tile):
            total = total + pieces[s]
        for n in range(n_pieces):
            grads_out[n] = total[:, n * 128 : n * 128 + 128]

    finish(quarter_copies)
    for m in range(tiles):
        placed_out[m] = quarter_recv[homes[m]]


def finish_kernel(placed, grads, join_sel, coarse, grad_conv, grad_bias, grad_down):
    local = coarse.shape[1]
    for n in range(coarse.shape[0]):
        for j in range(16):
            lanes = slice((j % 8) * 128, (j % 8) * 128 + 128)
            q = n * 4 + (j // 8) * 2
            both = jnp.concatenate([placed[q, :, lanes], placed[q + 1, :, lanes]], axis=1)
            coarse[n, :, 256 * j : 256 * j + 256] = dot(both, join_sel[...]).astype(BF16)
    whole = jnp.concatenate([grads[n] for n in range(grads.shape[0])], axis=1)
    grad_conv[...] = whole[:, : TAPS * C]
    grad_bias[...] = whole[:1, BIAS_COL : BIAS_COL + local]
    for n in range(C // local):
        col = DOWN_COL + n * 4 * local
        grad_down[n * local : (n + 1) * local] = whole[:, col : col + 4 * local]


def on_device(
    n_tile,
    n_chan,
    features,
    conv_weight,
    conv_bias,
    down_weight,
    cotangent,
    edge_links,
    edge_turns,
    corner_links,
    corner_turns,
    child_slot,
):
    tiles, local = features.shape[0], features.shape[1]
    per = tiles // n_chan
    n_pieces = PACK // 128
    hbm = pl.BlockSpec(memory_space=pl.ANY)
    vmem = pl.BlockSpec(memory_space=pltpu.VMEM)
    smem = pl.BlockSpec(memory_space=pltpu.SMEM)
    table = jnp.concatenate(
        [edge_links, edge_turns, corner_links, corner_turns, child_slot[:, None]], axis=1
    )
    table = jnp.pad(table, ((0, 0), (0, 128 - table.shape[1])))

    def const(values):
        return jnp.asarray(values, BF16)

    half = half_selector()
    selectors = [
        const(rim_selector()),
        const(half),
        const(phase_selector()),
        const(side_selector()),
        const(cap_selector()),
        const(tap_selector()),
        const(down_selector(n_chan)),
    ]
    split = n_tile == n_pieces
    piece_shape = (n_tile, local, 128 if split else PACK)
    dma = pltpu.SemaphoreType.DMA
    placed, grads = pl.pallas_call(
        functools.partial(level_kernel, n_tile, n_chan, tiles),
        out_shape=[
            jax.ShapeDtypeStruct((tiles, local, QUARTER), BF16),
            jax.ShapeDtypeStruct((n_pieces, local, 128), F32),
        ],
        in_specs=[hbm] * 12 + [smem],
        out_specs=[vmem] * 2,
        scratch_shapes=[
            pltpu.VMEM(features.shape, BF16),
            pltpu.VMEM(cotangent.shape, BF16),
        ]
        + [pltpu.VMEM(selector.shape, BF16) for selector in selectors]
        + [
            pltpu.VMEM((n_chan, per, local, S * S), BF16),
            pltpu.VMEM((n_chan, local, C * TAPS), BF16),
            pltpu.VMEM((n_chan, C, local * 4), BF16),
            pltpu.VMEM((n_chan, local, 128), F32),
            pltpu.VMEM((n_tile, tiles, 128), jnp.int32),
            pltpu.SMEM((n_tile, tiles, 128), jnp.int32),
            pltpu.VMEM((n_tile, tiles, local, 4 * S), BF16),
            pltpu.VMEM((tiles, local, 6 * S), BF16),
            pltpu.VMEM((n_chan, per, local, 6 * S), BF16),
            pltpu.VMEM((tiles, local, QUARTER), BF16),
            pltpu.VMEM((n_tile, local, QUARTER), BF16),
            pltpu.VMEM((n_tile, local, QUARTER), BF16),
            pltpu.VMEM((tiles, local, QUARTER), BF16),
            pltpu.VMEM((n_chan, per, local, QUARTER), BF16),
            pltpu.VMEM((4 * C, 16 * C), BF16),
            pltpu.VMEM((per, 4, C, QUARTER), F32),
            pltpu.VMEM((per, 16 * C, QUARTER), BF16),
            pltpu.VMEM((per, 4 * C, QUARTER), F32),
            pltpu.VMEM((per, 4 * C, QUARTER), BF16),
            pltpu.VMEM((per, C, QUARTER), BF16),
            pltpu.VMEM((n_chan, per, local, QUARTER), BF16),
            pltpu.VMEM((n_tile, local, QUARTER), BF16),
            pltpu.VMEM((n_tile, local, QUARTER), BF16),
            pltpu.VMEM((C, PACK), F32),
            pltpu.VMEM((n_chan, local, PACK), F32),
            pltpu.VMEM(piece_shape, F32),
            pltpu.VMEM((n_tile, local, 128), F32),
            dma((14,)),
            dma((8, n_chan)),
            dma((8, n_chan)),
            dma((5, n_tile)),
            dma((5, n_tile)),
            dma((2, n_tile // 2)),
            dma((2, n_tile // 2)),
        ],
        compiler_params=pltpu.CompilerParams(
            collective_id=0, has_side_effects=True, vmem_limit_bytes=VMEM_LIMIT
        ),
        name="unet_level",
    )(features, cotangent, conv_weight, down_weight, table, *selectors, conv_bias)
    coarse, grad_conv, grad_bias, grad_down = pl.pallas_call(
        finish_kernel,
        out_shape=[
            jax.ShapeDtypeStruct(cotangent.shape, BF16),
            jax.ShapeDtypeStruct(conv_weight.shape, F32),
            jax.ShapeDtypeStruct((1, local), F32),
            jax.ShapeDtypeStruct(down_weight.shape, F32),
        ],
        in_specs=[vmem] * 3,
        out_specs=[vmem] * 4,
        compiler_params=pltpu.CompilerParams(vmem_limit_bytes=VMEM_LIMIT),
        name="finish",
    )(placed, grads, const(half.T))
    return (coarse, grad_conv, grad_bias.reshape(local), grad_down)


def solution(mesh):
    n_tile, n_chan = mesh.shape["tile"], mesh.shape["chan"]
    in_specs = (
        P("tile", "chan", None),
        P("chan", None),
        P("chan"),
        P(None, "chan"),
        P("tile", "chan", None),
        P("tile", None),
        P("tile", None),
        P("tile", None),
        P("tile", None),
        P("tile"),
    )
    out_specs = (P("tile", "chan", None), P("chan", None), P("chan"), P(None, "chan"))
    return jax.shard_map(
        functools.partial(on_device, n_tile, n_chan),
        mesh=mesh,
        in_specs=in_specs,
        out_specs=out_specs,
        check_vma=False,
    )
```

```python
import functools

import jax
import jax.numpy as jnp
import numpy as np
from jax import lax
from jax.experimental import pallas as pl
from jax.experimental.pallas import tpu as pltpu
from jax.sharding import PartitionSpec as P

C = 64
S = 64
H = S // 2
QUARTER = H * H
TAPS = 9
MESH = pl.DeviceIdType.MESH
F32 = jnp.float32
BF16 = jnp.bfloat16
VMEM_LIMIT = 63 * 1024 * 1024
PACK = 1024
FEAT = 8
BIAS_COL = TAPS * C
DOWN_COL = BIAS_COL + C


def rim_selector():
    pick = np.zeros((S * S, 4 * S), np.float32)
    for n in range(S):
        pick[S - 1 - n, n] = 1
        pick[n * S, S + n] = 1
        pick[(S - 1) * S + n, 2 * S + n] = 1
        pick[(S - 1 - n) * S + S - 1, 3 * S + n] = 1
    return pick


def phase_selector():
    lane = np.arange(8 * S)
    row, col = lane // S, lane % S
    target = ((row % 2) * 2 + col % 2) * 128 + (row // 2) * H + col // 2
    pick = np.zeros((8 * S, 8 * S), np.float32)
    pick[lane, target] = 1
    return pick


def half_selector():
    lane = np.arange(4 * S)
    row, col = lane // S, lane % S
    pick = np.zeros((4 * S, 4 * S), np.float32)
    pick[lane, (col // H) * 128 + row * H + col % H] = 1
    return pick


def side_selector():
    pick = np.zeros((2 * S, 4 * QUARTER), np.float32)
    for a in range(2):
        for u in range(H):
            pick[S - 1 - (2 * u + a), a * QUARTER + u * H] = 1
            pick[S + 2 * u + a, (2 + a) * QUARTER + u * H + H - 1] = 1
    return pick


def cap_selector():
    pick = np.zeros((4 * S, 8 * 128), np.float32)
    for wx in range(4):
        for v in range(H):
            x = 2 * v + wx - 1
            top = 128 + 0 if x < 0 else 128 + 3 if x >= S else x
            low = 128 + 1 if x < 0 else 128 + 2 if x >= S else S + S - 1 - x
            pick[top, wx * 128 + v] = 1
            pick[low, (4 + wx) * 128 + 96 + v] = 1
    return pick


def tap_selector():
    pick = np.zeros((C * TAPS, C * TAPS), np.float32)
    for i in range(C):
        for tap in range(TAPS):
            pick[i * TAPS + tap, tap * C + i] = 1
    return pick


def down_selector(n_chan):
    local = C // n_chan
    pick = np.zeros((n_chan, local * 4, C * 4), np.float32)
    for i in range(C):
        for ab in range(4):
            pick[i // local, (i % local) * 4 + ab, ab * C + i] = 1
    return pick


def dot(a, b):
    return jnp.dot(a, b, preferred_element_type=F32)


def dot_nt(a, b):
    return lax.dot_general(a, b, (((1,), (1,)), ((), ())), preferred_element_type=F32)


def split_dot_nt(a, selector):
    high = a.astype(BF16)
    rest = a - high.astype(F32)
    middle = rest.astype(BF16)
    low = (rest - middle.astype(F32)).astype(BF16)
    return dot_nt(high, selector) + dot_nt(middle, selector) + dot_nt(low, selector)


def greet(n_tile, n_chan, me_t, me_c):
    barrier = pltpu.get_barrier_semaphore()
    for k in range(1, n_tile):
        peer = lax.rem(me_t + k, n_tile)
        pl.semaphore_signal(barrier, inc=1, device_id=(peer, me_c), device_id_type=MESH)
    for k in range(1, n_chan):
        peer = lax.rem(me_c + k, n_chan)
        pl.semaphore_signal(barrier, inc=1, device_id=(me_t, peer), device_id_type=MESH)


def remote(src, dst, send_sem, recv_sem, device):
    copy = pltpu.make_async_remote_copy(
        src_ref=src,
        dst_ref=dst,
        send_sem=send_sem,
        recv_sem=recv_sem,
        device_id=device,
        device_id_type=MESH,
    )
    copy.start()
    return copy


def find_owners(table, groups, tiles, wanted):
    def step(s, found):
        for t in range(tiles):
            value = table[s, t, 0]
            found = tuple(jnp.where(value == w, s, f) for w, f in zip(wanted, found))
        return found

    return lax.fori_loop(0, groups, step, (jnp.int32(0),) * len(wanted))


def widen_weights(taps, wide):
    none = jnp.zeros((C, C), F32)
    for a in range(2):
        for b in range(2):
            pieces = []
            for wy in range(4):
                for wx in range(4):
                    dy, dx = wy - a, wx - b
                    if 0 <= dy < 3 and 0 <= dx < 3:
                        tap = 3 * dy + dx
                        pieces.append(taps[:, tap * C : tap * C + C])
                    else:
                        pieces.append(none)
            row = (a * 2 + b) * C
            wide[row : row + C, :] = jnp.concatenate(pieces, axis=1).astype(BF16)


def fill_window(phase, sides, caps, window, t):
    lane = lax.broadcasted_iota(jnp.int32, (C, QUARTER), 1)
    first_col = lax.rem(lane, H) == 0
    last_col = lax.rem(lane, H) == H - 1
    lane_cap = lax.broadcasted_iota(jnp.int32, (C, 128), 1)
    for a in range(2):
        even, odd = phase[a * 2], phase[a * 2 + 1]
        west = jnp.where(
            first_col, sides[:, a * QUARTER : (a + 1) * QUARTER], pltpu.roll(odd, 1, 1)
        )
        east = jnp.where(
            last_col,
            sides[:, (2 + a) * QUARTER : (3 + a) * QUARTER],
            pltpu.roll(even, QUARTER - 1, 1),
        )
        for wx, middle in enumerate((west, even, odd, east)):
            row = ((1 + a) * 4 + wx) * C
            window[t, row : row + C, :] = middle.astype(BF16)
            if a == 1:
                moved = pltpu.roll(middle, H, 1)
                cap = caps[:, wx * 128 : wx * 128 + 128]
                head = jnp.where(lane_cap < H, cap, moved[:, :128])
                moved = jnp.concatenate([head, moved[:, 128:]], axis=1)
                row = wx * C
            else:
                moved = pltpu.roll(middle, QUARTER - H, 1)
                cap = caps[:, (4 + wx) * 128 : (5 + wx) * 128]
                tail = jnp.where(lane_cap >= 128 - H, cap, moved[:, QUARTER - 128 :])
                moved = jnp.concatenate([moved[:, : QUARTER - 128], tail], axis=1)
                row = (12 + wx) * C
            window[t, row : row + C, :] = moved.astype(BF16)


def level_kernel(
    n_tile,
    n_chan,
    tiles,
    feat_hbm,
    cot_hbm,
    cw_hbm,
    dw_hbm,
    rim_sel_hbm,
    half_sel_hbm,
    phase_sel_hbm,
    side_sel_hbm,
    cap_sel_hbm,
    tap_sel_hbm,
    down_sel_hbm,
    cb_smem,
    el_smem,
    et_smem,
    cl_smem,
    ct_smem,
    slot_smem,
    placed_out,
    grads_out,
    feat,
    cot,
    rim_sel,
    half_sel,
    phase_sel,
    side_sel,
    cap_sel,
    tap_sel,
    down_sel,
    feat_all,
    cw_all,
    dw_all,
    cb_all,
    table_all,
    table,
    rims,
    halos,
    halo_all,
    slots,
    cot_send,
    cot_recv,
    cot_group,
    cot_all,
    wide,
    phases,
    window,
    slope,
    hidden,
    quarter,
    quarter_group,
    quarter_send,
    quarter_recv,
    pack,
    pack_recv,
    pieces,
    pieces_recv,
    local_sem,
    chan_send,
    chan_recv,
    tile_send,
    tile_recv,
    rim_send,
    rim_recv,
):
    me_t = lax.axis_index("tile")
    me_c = lax.axis_index("chan")
    per = tiles // n_chan
    local = feat.shape[1]
    n_outer = n_tile // 2
    outer, inner = me_t // 2, lax.rem(me_t, 2)

    greet(n_tile, n_chan, me_t, me_c)

    def fetch(src, dst, k):
        copy = pltpu.make_async_copy(src, dst, local_sem.at[k])
        copy.start()
        return copy

    get_feat = fetch(feat_hbm, feat, 0)
    get_rim_sel = fetch(rim_sel_hbm, rim_sel, 1)
    get_cot = fetch(cot_hbm, cot, 2)
    get_half_sel = fetch(half_sel_hbm, half_sel, 3)
    get_own = [
        fetch(cw_hbm, cw_all.at[me_c], 5),
        fetch(dw_hbm, dw_all.at[me_c], 6),
        fetch(feat_hbm.at[pl.ds(me_c * per, per)], feat_all.at[me_c], 4),
        fetch(phase_sel_hbm, phase_sel, 8),
        fetch(side_sel_hbm, side_sel, 9),
        fetch(cap_sel_hbm, cap_sel, 10),
        fetch(tap_sel_hbm, tap_sel, 11),
        fetch(down_sel_hbm, down_sel, 12),
    ]
    row = lax.broadcasted_iota(jnp.int32, (local, 128), 0)
    bias = jnp.zeros((local, 128), F32)
    for n in range(local):
        bias = jnp.where(row == n, cb_smem[n], bias)
    cb_all[pl.ds(me_c, 1)] = bias[None]
    row = lax.broadcasted_iota(jnp.int32, (tiles, 128), 0)
    own_slots = jnp.zeros((tiles, 128), jnp.int32)
    for t in range(tiles):
        own_slots = jnp.where(row == t, slot_smem[0, t], own_slots)
    table_all[pl.ds(me_t, 1)] = own_slots[None]

    get_feat.wait()
    get_rim_sel.wait()
    pixels = feat[...].reshape(tiles * local, S * S)
    my_rims = dot(pixels, rim_sel[...]).astype(BF16)
    rims[pl.ds(me_t, 1)] = my_rims.reshape(1, tiles, local, 4 * S)

    pl.semaphore_wait(pltpu.get_barrier_semaphore(), n_tile - 1 + n_chan - 1)

    def to_tiles(kind, src, dst):
        copies = []
        for k in range(1, n_tile):
            d = lax.rem(me_t + k, n_tile)
            copies.append(
                remote(
                    src(d), dst, tile_send.at[kind, k], tile_recv.at[kind, k], (d, me_c)
                )
            )
        return copies

    def to_chans(kind, src, dst):
        copies = []
        for k in range(1, n_chan):
            c = lax.rem(me_c + k, n_chan)
            copies.append(
                remote(
                    src(c), dst, chan_send.at[kind, k], chan_recv.at[kind, k], (me_t, c)
                )
            )
        return copies

    def finish(copies):
        for copy in copies:
            copy.wait()

    def chan_rows(c):
        return pl.ds(pl.multiple_of(c * local, local), local)

    table_copies = to_tiles(0, lambda d: table_all.at[me_t], table_all.at[me_t])
    across = outer * 2 + 1 - inner
    forwards = [
        remote(
            rims.at[me_t], rims.at[me_t], rim_send.at[1, 0], rim_recv.at[1, 0], (across, me_c)
        )
    ]
    straight = []
    for k in range(1, n_outer):
        d = lax.rem(outer + k, n_outer) * 2 + inner
        straight.append(
            remote(rims.at[me_t], rims.at[me_t], rim_send.at[0, k], rim_recv.at[0, k], (d, me_c))
        )
    small_copies = (
        to_chans(1, lambda c: cw_hbm, cw_all.at[me_c])
        + to_chans(2, lambda c: dw_hbm, dw_all.at[me_c])
        + to_chans(3, lambda c: cb_all.at[me_c], cb_all.at[me_c])
    )
    feat_copies = [
        to_chans(FEAT + t, lambda c: feat_hbm.at[c * per + t], feat_all.at[me_c, t])
        for t in range(per)
    ]

    get_cot.wait()
    get_half_sel.wait()
    coarse_tiles = cot.shape[0]
    cots = cot[...].reshape(coarse_tiles * local, S * S)
    for j in range(16):
        moved = dot(cots[:, 256 * j : 256 * j + 256], half_sel[...]).astype(BF16)
        lanes = slice((j % 8) * 128, (j % 8) * 128 + 128)
        for n in range(coarse_tiles):
            rows = moved[n * local : (n + 1) * local]
            slots[n * 4 + (j // 8) * 2, :, lanes] = rows[:, :128]
            slots[n * 4 + (j // 8) * 2 + 1, :, lanes] = rows[:, 128:]

    finish(table_copies)
    to_smem = pltpu.make_async_copy(table_all, table, local_sem.at[7])
    to_smem.start()
    to_smem.wait()
    homes = find_owners(table, n_tile, tiles, tuple(me_t * tiles + m for m in range(tiles)))
    owners = [slot_smem[0, t] // tiles for t in range(tiles)]
    for d in range(n_tile):
        chosen = jnp.int32(0)
        for m in range(tiles):
            chosen = jnp.where(homes[m] == d, m, chosen)
        cot_send[d] = slots[chosen]
    cot_recv[pl.ds(me_t, 1)] = cot_send[pl.ds(me_t, 1)]

    for k in range(1, n_outer):
        straight[k - 1].wait_recv()
        source = lax.rem(outer + n_outer - k, n_outer) * 2 + inner
        forwards.append(
            remote(
                rims.at[source],
                rims.at[source],
                rim_send.at[1, k],
                rim_recv.at[1, k],
                (across, me_c),
            )
        )
    cot_copies = to_tiles(1, lambda d: cot_send.at[d], cot_recv.at[me_t])

    finish(get_own)
    finish(small_copies)
    widen_weights(dot(cw_all[...].reshape(C, C * TAPS), tap_sel[...]), wide)
    down = jnp.zeros((C, 4 * C), F32)
    for c in range(n_chan):
        down = down + dot(dw_all[c], down_sel[c])
    down_t = down.T.astype(BF16)
    down = down.astype(BF16)

    def deinterleave(t):
        finish(feat_copies[t])
        pixels = feat_all[:, t].reshape(C, S * S)
        for j in range(8):
            moved = dot(pixels[:, 512 * j : 512 * j + 512], phase_sel[...])
            for p in range(4):
                phases[t, p, :, 128 * j : 128 * j + 128] = moved[:, p * 128 : p * 128 + 128]

    deinterleave(0)
    finish(forwards)
    for copy in straight:
        copy.wait_send()
    lane = lax.broadcasted_iota(jnp.int32, (local, 128), 1)
    for t in range(tiles):
        strips = []
        corners = jnp.zeros((local, 128), F32)
        for k in range(4):
            link = el_smem[k, t]
            chosen = lax.rem(k + 2 + et_smem[k, t], 4)
            block = rims[link // tiles, lax.rem(link, tiles)].astype(F32)
            strip = block[:, :S]
            for r in range(1, 4):
                strip = jnp.where(chosen == r, block[:, r * S : r * S + S], strip)
            strips.append(strip)
            link = cl_smem[k, t]
            chosen = lax.rem(k + 3 + ct_smem[k, t], 4)
            held = jnp.maximum(link, 0)
            block = rims[held // tiles, lax.rem(held, tiles)].astype(F32)
            value = block[:, :1]
            for r in range(1, 4):
                value = jnp.where(chosen == r, block[:, r * S : r * S + 1], value)
            value = jnp.where(link >= 0, value, jnp.zeros_like(value))
            corners = jnp.where(lane == k, value, corners)
        north, west, south, east = strips
        halos[t] = jnp.concatenate([west, east, north, south, corners], axis=1).astype(BF16)
    halo_all[pl.ds(me_c, 1)] = halos[pl.ds(me_c * per, per)][None]
    halo_copies = to_chans(4, lambda c: halos.at[pl.ds(c * per, per)], halo_all.at[me_c])

    finish(cot_copies)
    for t in range(tiles):
        cot_group[t] = cot_recv[owners[t]]
    cot_all[pl.ds(me_c, 1)] = cot_group[pl.ds(me_c * per, per)][None]
    cot_chan_copies = to_chans(
        6, lambda c: cot_group.at[pl.ds(c * per, per)], cot_all.at[me_c]
    )

    for t in range(1, per):
        deinterleave(t)
    finish(halo_copies)
    bias = jnp.concatenate([cb_all[...].reshape(C, 128)[:, :1]] * 4, axis=0)
    quarter_copies = []
    for t in range(per):
        halo = halo_all[:, t].reshape(C, 6 * S)
        sides = dot(halo[:, : 2 * S], side_sel[...])
        caps = dot(halo[:, 2 * S :], cap_sel[...])
        fill_window([phases[t, p] for p in range(4)], sides, caps, window, t)
        pre = dot(wide[...], window[t]) + bias
        squashed = 1.0 / (1.0 + jnp.exp(-pre))
        slope[t] = squashed * (1.0 + pre * (1.0 - squashed))
        hidden[t] = (pre * squashed).astype(BF16)
        quarter[t] = dot(down, hidden[t]).astype(BF16)
        quarter_group[pl.ds(me_c, 1), t] = quarter[t, chan_rows(me_c)][None]
        quarter_copies += to_chans(
            FEAT + per + t, lambda c: quarter.at[t, chan_rows(c)], quarter_group.at[me_c, t]
        )

    finish(quarter_copies)
    for d in range(n_tile):
        chosen = jnp.int32(0)
        for t in range(tiles):
            chosen = jnp.where(owners[t] == d, t, chosen)
        quarter_send[d] = quarter_group[chosen // per, lax.rem(chosen, per)]
    quarter_recv[pl.ds(me_t, 1)] = quarter_send[pl.ds(me_t, 1)]
    quarter_copies = to_tiles(2, lambda d: quarter_send.at[d], quarter_recv.at[me_t])

    finish(cot_chan_copies)
    grad_wide = jnp.zeros((4 * C, 16 * C), F32)
    grad_down = jnp.zeros((C, 4 * C), F32)
    grad_bias = jnp.zeros((8, 4 * C), F32)
    ones = jnp.ones((8, QUARTER), BF16)
    for t in range(per):
        back = cot_all[:, t].reshape(C, QUARTER)
        grad_pre = (dot(down_t, back) * slope[t]).astype(BF16)
        grad_down = grad_down + dot_nt(back, hidden[t])
        grad_bias = grad_bias + dot_nt(ones, grad_pre)
        grad_wide = grad_wide + dot_nt(grad_pre, window[t])
    taps = []
    for dy in range(3):
        for dx in range(3):
            total = jnp.zeros((C, C), F32)
            for a in range(2):
                for b in range(2):
                    row = (a * 2 + b) * C
                    col = ((a + dy) * 4 + b + dx) * C
                    total = total + grad_wide[row : row + C, col : col + C]
            taps.append(total)
    pack[:, : TAPS * C] = split_dot_nt(jnp.concatenate(taps, axis=1), tap_sel[...])
    pack[:, TAPS * C :] = jnp.zeros((C, PACK - TAPS * C), F32)
    grad_down = split_dot_nt(grad_down, down_sel[...].reshape(4 * C, 4 * C))
    total = grad_bias[:1, :C]
    for ab in range(1, 4):
        total = total + grad_bias[:1, ab * C : ab * C + C]
    for c in range(n_chan):
        rows = slice(c * local, c * local + local)
        pack[c * local : c * local + 1, BIAS_COL : BIAS_COL + local] = total[:, rows]
        wide_cols = slice(c * 4 * local, (c + 1) * 4 * local)
        for n in range(C // local):
            col = DOWN_COL + n * 4 * local
            pack[rows, col : col + 4 * local] = grad_down[n * local : (n + 1) * local, wide_cols]

    pack_recv[pl.ds(me_c, 1)] = pack[chan_rows(me_c)][None]
    finish(to_chans(7, lambda c: pack.at[chan_rows(c)], pack_recv.at[me_c]))
    total = pack_recv[0]
    for c in range(1, n_chan):
        total = total + pack_recv[c]
    n_pieces = PACK // 128
    if n_tile == n_pieces:
        for n in range(n_pieces):
            pieces[n] = total[:, n * 128 : n * 128 + 128]
        pieces_recv[pl.ds(me_t, 1)] = pieces[pl.ds(me_t, 1)]
        finish(to_tiles(3, lambda d: pieces.at[d], pieces_recv.at[me_t]))
        total = pieces_recv[0]
        for s in range(1, n_tile):
            total = total + pieces_recv[s]
        grads_out[pl.ds(me_t, 1)] = total[None]
        finish(to_tiles(4, lambda d: grads_out.at[me_t], grads_out.at[me_t]))
    else:
        pieces[pl.ds(me_t, 1)] = total[None]
        finish(to_tiles(3, lambda d: pieces.at[me_t], pieces.at[me_t]))
        total = pieces[0]
        for s in range(1, n_tile):
            total = total + pieces[s]
        for n in range(n_pieces):
            grads_out[n] = total[:, n * 128 : n * 128 + 128]

    finish(quarter_copies)
    for m in range(tiles):
        placed_out[m] = quarter_recv[homes[m]]


def finish_kernel(placed, grads, join_sel, coarse, grad_conv, grad_bias, grad_down):
    local = coarse.shape[1]
    for n in range(coarse.shape[0]):
        for j in range(16):
            lanes = slice((j % 8) * 128, (j % 8) * 128 + 128)
            q = n * 4 + (j // 8) * 2
            both = jnp.concatenate([placed[q, :, lanes], placed[q + 1, :, lanes]], axis=1)
            coarse[n, :, 256 * j : 256 * j + 256] = dot(both, join_sel[...]).astype(BF16)
    whole = jnp.concatenate([grads[n] for n in range(grads.shape[0])], axis=1)
    grad_conv[...] = whole[:, : TAPS * C]
    grad_bias[...] = whole[:1, BIAS_COL : BIAS_COL + local]
    for n in range(C // local):
        col = DOWN_COL + n * 4 * local
        grad_down[n * local : (n + 1) * local] = whole[:, col : col + 4 * local]


def on_device(
    n_tile,
    n_chan,
    features,
    conv_weight,
    conv_bias,
    down_weight,
    cotangent,
    edge_links,
    edge_turns,
    corner_links,
    corner_turns,
    child_slot,
):
    tiles, local = features.shape[0], features.shape[1]
    per = tiles // n_chan
    n_pieces = PACK // 128
    hbm = pl.BlockSpec(memory_space=pltpu.HBM)
    vmem = pl.BlockSpec(memory_space=pltpu.VMEM)
    smem = pl.BlockSpec(memory_space=pltpu.SMEM)
    tables = [edge_links.T, edge_turns.T, corner_links.T, corner_turns.T, child_slot[None]]

    def const(values):
        return jnp.asarray(values, BF16)

    half = half_selector()
    selectors = [
        const(rim_selector()),
        const(half),
        const(phase_selector()),
        const(side_selector()),
        const(cap_selector()),
        const(tap_selector()),
        const(down_selector(n_chan)),
    ]
    split = n_tile == n_pieces
    piece_shape = (n_tile, local, 128 if split else PACK)
    dma = pltpu.SemaphoreType.DMA
    placed, grads = pl.pallas_call(
        functools.partial(level_kernel, n_tile, n_chan, tiles),
        out_shape=[
            jax.ShapeDtypeStruct((tiles, local, QUARTER), BF16),
            jax.ShapeDtypeStruct((n_pieces, local, 128), F32),
        ],
        in_specs=[hbm] * 11 + [smem] * 6,
        out_specs=[vmem] * 2,
        scratch_shapes=[
            pltpu.VMEM(features.shape, BF16),
            pltpu.VMEM(cotangent.shape, BF16),
        ]
        + [pltpu.VMEM(selector.shape, BF16) for selector in selectors]
        + [
            pltpu.VMEM((n_chan, per, local, S * S), BF16),
            pltpu.VMEM((n_chan, local, C * TAPS), BF16),
            pltpu.VMEM((n_chan, C, local * 4), BF16),
            pltpu.VMEM((n_chan, local, 128), F32),
            pltpu.VMEM((n_tile, tiles, 128), jnp.int32),
            pltpu.SMEM((n_tile, tiles, 128), jnp.int32),
            pltpu.VMEM((n_tile, tiles, local, 4 * S), BF16),
            pltpu.VMEM((tiles, local, 6 * S), BF16),
            pltpu.VMEM((n_chan, per, local, 6 * S), BF16),
            pltpu.VMEM((tiles, local, QUARTER), BF16),
            pltpu.VMEM((n_tile, local, QUARTER), BF16),
            pltpu.VMEM((n_tile, local, QUARTER), BF16),
            pltpu.VMEM((tiles, local, QUARTER), BF16),
            pltpu.VMEM((n_chan, per, local, QUARTER), BF16),
            pltpu.VMEM((4 * C, 16 * C), BF16),
            pltpu.VMEM((per, 4, C, QUARTER), F32),
            pltpu.VMEM((per, 16 * C, QUARTER), BF16),
            pltpu.VMEM((per, 4 * C, QUARTER), F32),
            pltpu.VMEM((per, 4 * C, QUARTER), BF16),
            pltpu.VMEM((per, C, QUARTER), BF16),
            pltpu.VMEM((n_chan, per, local, QUARTER), BF16),
            pltpu.VMEM((n_tile, local, QUARTER), BF16),
            pltpu.VMEM((n_tile, local, QUARTER), BF16),
            pltpu.VMEM((C, PACK), F32),
            pltpu.VMEM((n_chan, local, PACK), F32),
            pltpu.VMEM(piece_shape, F32),
            pltpu.VMEM((n_tile, local, 128), F32),
            dma((13,)),
            dma((FEAT + 2 * per, n_chan)),
            dma((FEAT + 2 * per, n_chan)),
            dma((5, n_tile)),
            dma((5, n_tile)),
            dma((2, n_tile // 2)),
            dma((2, n_tile // 2)),
        ],
        compiler_params=pltpu.CompilerParams(
            collective_id=0, has_side_effects=True, vmem_limit_bytes=VMEM_LIMIT
        ),
        name="unet_level",
    )(features, cotangent, conv_weight, down_weight, *selectors, conv_bias, *tables)
    coarse, grad_conv, grad_bias, grad_down = pl.pallas_call(
        finish_kernel,
        out_shape=[
            jax.ShapeDtypeStruct(cotangent.shape, BF16),
            jax.ShapeDtypeStruct(conv_weight.shape, F32),
            jax.ShapeDtypeStruct((1, local), F32),
            jax.ShapeDtypeStruct(down_weight.shape, F32),
        ],
        in_specs=[vmem] * 3,
        out_specs=[vmem] * 4,
        compiler_params=pltpu.CompilerParams(vmem_limit_bytes=VMEM_LIMIT),
        name="finish",
    )(placed, grads, const(half.T))
    return (coarse, grad_conv, grad_bias.reshape(local), grad_down)


def solution(mesh):
    n_tile, n_chan = mesh.shape["tile"], mesh.shape["chan"]
    in_specs = (
        P("tile", "chan", None),
        P("chan", None),
        P("chan"),
        P(None, "chan"),
        P("tile", "chan", None),
        P("tile", None),
        P("tile", None),
        P("tile", None),
        P("tile", None),
        P("tile"),
    )
    out_specs = (P("tile", "chan", None), P("chan", None), P("chan"), P(None, "chan"))
    return jax.shard_map(
        functools.partial(on_device, n_tile, n_chan),
        mesh=mesh,
        in_specs=in_specs,
        out_specs=out_specs,
        check_vma=False,
    )
```

```python
import functools

import jax
import jax.numpy as jnp
import numpy as np
from jax import lax
from jax.experimental import pallas as pl
from jax.experimental.pallas import tpu as pltpu
from jax.sharding import PartitionSpec as P

C = 64
S = 64
H = S // 2
QUARTER = H * H
TAPS = 9
MESH = pl.DeviceIdType.MESH
F32 = jnp.float32
BF16 = jnp.bfloat16
VMEM_LIMIT = 63 * 1024 * 1024
PACK = 1024
FEAT = 8
BIAS_COL = TAPS * C
DOWN_COL = BIAS_COL + C


def rim_selector():
    pick = np.zeros((S * S, 4 * S), np.float32)
    for n in range(S):
        pick[S - 1 - n, n] = 1
        pick[n * S, S + n] = 1
        pick[(S - 1) * S + n, 2 * S + n] = 1
        pick[(S - 1 - n) * S + S - 1, 3 * S + n] = 1
    return pick


def phase_selector():
    lane = np.arange(8 * S)
    row, col = lane // S, lane % S
    target = ((row % 2) * 2 + col % 2) * 128 + (row // 2) * H + col // 2
    pick = np.zeros((8 * S, 8 * S), np.float32)
    pick[lane, target] = 1
    return pick


def half_selector():
    lane = np.arange(4 * S)
    row, col = lane // S, lane % S
    pick = np.zeros((4 * S, 4 * S), np.float32)
    pick[lane, (col // H) * 128 + row * H + col % H] = 1
    return pick


def side_selector():
    pick = np.zeros((2 * S, 4 * QUARTER), np.float32)
    for a in range(2):
        for u in range(H):
            pick[S - 1 - (2 * u + a), a * QUARTER + u * H] = 1
            pick[S + 2 * u + a, (2 + a) * QUARTER + u * H + H - 1] = 1
    return pick


def cap_selector():
    pick = np.zeros((4 * S, 8 * 128), np.float32)
    for wx in range(4):
        for v in range(H):
            x = 2 * v + wx - 1
            top = 128 + 0 if x < 0 else 128 + 3 if x >= S else x
            low = 128 + 1 if x < 0 else 128 + 2 if x >= S else S + S - 1 - x
            pick[top, wx * 128 + v] = 1
            pick[low, (4 + wx) * 128 + 96 + v] = 1
    return pick


def tap_selector():
    pick = np.zeros((C * TAPS, C * TAPS), np.float32)
    for i in range(C):
        for tap in range(TAPS):
            pick[i * TAPS + tap, tap * C + i] = 1
    return pick


def down_selector(n_chan):
    local = C // n_chan
    pick = np.zeros((n_chan, local * 4, C * 4), np.float32)
    for i in range(C):
        for ab in range(4):
            pick[i // local, (i % local) * 4 + ab, ab * C + i] = 1
    return pick


def dot(a, b):
    return jnp.dot(a, b, preferred_element_type=F32)


def dot_nt(a, b):
    return lax.dot_general(a, b, (((1,), (1,)), ((), ())), preferred_element_type=F32)


def split_dot_nt(a, selector):
    high = a.astype(BF16)
    rest = a - high.astype(F32)
    middle = rest.astype(BF16)
    low = (rest - middle.astype(F32)).astype(BF16)
    rows = a.shape[0]
    moved = dot_nt(jnp.concatenate([high, middle, low], axis=0), selector)
    return moved[:rows] + moved[rows : 2 * rows] + moved[2 * rows :]


def greet(n_tile, n_chan, me_t, me_c):
    barrier = pltpu.get_barrier_semaphore()
    for k in range(1, n_tile):
        peer = lax.rem(me_t + k, n_tile)
        pl.semaphore_signal(barrier, inc=1, device_id=(peer, me_c), device_id_type=MESH)
    for k in range(1, n_chan):
        peer = lax.rem(me_c + k, n_chan)
        pl.semaphore_signal(barrier, inc=1, device_id=(me_t, peer), device_id_type=MESH)


def remote(src, dst, send_sem, recv_sem, device):
    copy = pltpu.make_async_remote_copy(
        src_ref=src,
        dst_ref=dst,
        send_sem=send_sem,
        recv_sem=recv_sem,
        device_id=device,
        device_id_type=MESH,
    )
    copy.start()
    return copy


def find_owners(table, groups, tiles, wanted):
    def step(s, found):
        for t in range(tiles):
            value = table[s, t, 0]
            found = tuple(jnp.where(value == w, s, f) for w, f in zip(wanted, found))
        return found

    return lax.fori_loop(0, groups, step, (jnp.int32(0),) * len(wanted))


def widen_weights(taps, wide):
    none = jnp.zeros((C, C), F32)
    for a in range(2):
        for b in range(2):
            pieces = []
            for wy in range(4):
                for wx in range(4):
                    dy, dx = wy - a, wx - b
                    if 0 <= dy < 3 and 0 <= dx < 3:
                        tap = 3 * dy + dx
                        pieces.append(taps[:, tap * C : tap * C + C])
                    else:
                        pieces.append(none)
            row = (a * 2 + b) * C
            wide[row : row + C, :] = jnp.concatenate(pieces, axis=1).astype(BF16)


def fill_window(phase, sides, caps, window, t):
    lane = lax.broadcasted_iota(jnp.int32, (C, QUARTER), 1)
    first_col = lax.rem(lane, H) == 0
    last_col = lax.rem(lane, H) == H - 1
    lane_cap = lax.broadcasted_iota(jnp.int32, (C, 128), 1)
    for a in range(2):
        even, odd = phase[a * 2], phase[a * 2 + 1]
        west = jnp.where(
            first_col, sides[:, a * QUARTER : (a + 1) * QUARTER], pltpu.roll(odd, 1, 1)
        )
        east = jnp.where(
            last_col,
            sides[:, (2 + a) * QUARTER : (3 + a) * QUARTER],
            pltpu.roll(even, QUARTER - 1, 1),
        )
        for wx, middle in enumerate((west, even, odd, east)):
            row = ((1 + a) * 4 + wx) * C
            window[t, row : row + C, :] = middle.astype(BF16)
            if a == 1:
                moved = pltpu.roll(middle, H, 1)
                cap = caps[:, wx * 128 : wx * 128 + 128]
                head = jnp.where(lane_cap < H, cap, moved[:, :128])
                moved = jnp.concatenate([head, moved[:, 128:]], axis=1)
                row = wx * C
            else:
                moved = pltpu.roll(middle, QUARTER - H, 1)
                cap = caps[:, (4 + wx) * 128 : (5 + wx) * 128]
                tail = jnp.where(lane_cap >= 128 - H, cap, moved[:, QUARTER - 128 :])
                moved = jnp.concatenate([moved[:, : QUARTER - 128], tail], axis=1)
                row = (12 + wx) * C
            window[t, row : row + C, :] = moved.astype(BF16)


def level_kernel(
    n_tile,
    n_chan,
    tiles,
    feat_hbm,
    cot_hbm,
    cw_hbm,
    dw_hbm,
    rim_sel_hbm,
    half_sel_hbm,
    phase_sel_hbm,
    side_sel_hbm,
    cap_sel_hbm,
    tap_sel_hbm,
    down_sel_hbm,
    cb_smem,
    el_smem,
    et_smem,
    cl_smem,
    ct_smem,
    slot_smem,
    placed_out,
    grads_out,
    feat,
    cot,
    rim_sel,
    half_sel,
    phase_sel,
    side_sel,
    cap_sel,
    tap_sel,
    down_sel,
    feat_all,
    cw_all,
    dw_all,
    cb_all,
    table_all,
    table,
    rims,
    halos,
    halo_all,
    slots,
    cot_send,
    cot_recv,
    cot_group,
    cot_all,
    wide,
    phases,
    window,
    slope,
    hidden,
    quarter,
    quarter_group,
    quarter_send,
    quarter_recv,
    pack,
    pack_recv,
    pieces,
    pieces_recv,
    local_sem,
    chan_send,
    chan_recv,
    tile_send,
    tile_recv,
    rim_send,
    rim_recv,
):
    me_t = lax.axis_index("tile")
    me_c = lax.axis_index("chan")
    per = tiles // n_chan
    local = feat.shape[1]
    n_outer = n_tile // 2
    outer, inner = me_t // 2, lax.rem(me_t, 2)

    greet(n_tile, n_chan, me_t, me_c)

    def fetch(src, dst, k):
        copy = pltpu.make_async_copy(src, dst, local_sem.at[k])
        copy.start()
        return copy

    get_feat = fetch(feat_hbm, feat, 0)
    get_rim_sel = fetch(rim_sel_hbm, rim_sel, 1)
    get_cot = fetch(cot_hbm, cot, 2)
    get_half_sel = fetch(half_sel_hbm, half_sel, 3)
    get_own = [
        fetch(cw_hbm, cw_all.at[me_c], 5),
        fetch(dw_hbm, dw_all.at[me_c], 6),
        fetch(feat_hbm.at[pl.ds(me_c * per, per)], feat_all.at[me_c], 4),
        fetch(phase_sel_hbm, phase_sel, 8),
        fetch(side_sel_hbm, side_sel, 9),
        fetch(cap_sel_hbm, cap_sel, 10),
        fetch(tap_sel_hbm, tap_sel, 11),
        fetch(down_sel_hbm, down_sel, 12),
    ]
    row = lax.broadcasted_iota(jnp.int32, (local, 128), 0)
    bias = jnp.zeros((local, 128), F32)
    for n in range(local):
        bias = jnp.where(row == n, cb_smem[n], bias)
    cb_all[pl.ds(me_c, 1)] = bias[None]
    row = lax.broadcasted_iota(jnp.int32, (tiles, 128), 0)
    own_slots = jnp.zeros((tiles, 128), jnp.int32)
    for t in range(tiles):
        own_slots = jnp.where(row == t, slot_smem[0, t], own_slots)
    table_all[pl.ds(me_t, 1)] = own_slots[None]

    pl.semaphore_wait(pltpu.get_barrier_semaphore(), n_tile - 1 + n_chan - 1)

    def to_tiles(kind, src, dst):
        copies = []
        for k in range(1, n_tile):
            d = lax.rem(me_t + k, n_tile)
            copies.append(
                remote(
                    src(d), dst, tile_send.at[kind, k], tile_recv.at[kind, k], (d, me_c)
                )
            )
        return copies

    def to_chans(kind, src, dst):
        copies = []
        for k in range(1, n_chan):
            c = lax.rem(me_c + k, n_chan)
            copies.append(
                remote(
                    src(c), dst, chan_send.at[kind, k], chan_recv.at[kind, k], (me_t, c)
                )
            )
        return copies

    def finish(copies):
        for copy in copies:
            copy.wait()

    def chan_rows(c):
        return pl.ds(pl.multiple_of(c * local, local), local)

    table_copies = to_tiles(0, lambda d: table_all.at[me_t], table_all.at[me_t])
    small_copies = (
        to_chans(1, lambda c: cw_hbm, cw_all.at[me_c])
        + to_chans(2, lambda c: dw_hbm, dw_all.at[me_c])
        + to_chans(3, lambda c: cb_all.at[me_c], cb_all.at[me_c])
    )
    feat_copies = [
        to_chans(FEAT + t, lambda c: feat_hbm.at[c * per + t], feat_all.at[me_c, t])
        for t in range(per)
    ]

    get_feat.wait()
    get_rim_sel.wait()
    pixels = feat[...].reshape(tiles * local, S * S)
    my_rims = dot(pixels, rim_sel[...]).astype(BF16)
    rims[pl.ds(me_t, 1)] = my_rims.reshape(1, tiles, local, 4 * S)
    across = outer * 2 + 1 - inner
    forwards = [
        remote(
            rims.at[me_t], rims.at[me_t], rim_send.at[1, 0], rim_recv.at[1, 0], (across, me_c)
        )
    ]
    straight = []
    for k in range(1, n_outer):
        d = lax.rem(outer + k, n_outer) * 2 + inner
        straight.append(
            remote(rims.at[me_t], rims.at[me_t], rim_send.at[0, k], rim_recv.at[0, k], (d, me_c))
        )

    get_cot.wait()
    get_half_sel.wait()
    coarse_tiles = cot.shape[0]
    cots = cot[...].reshape(coarse_tiles * local, S * S)
    chunks = [cots[:, 256 * j : 256 * j + 256] for j in range(16)]
    moved = dot(jnp.concatenate(chunks, axis=0), half_sel[...]).astype(BF16)
    for j in range(16):
        lanes = slice((j % 8) * 128, (j % 8) * 128 + 128)
        for n in range(coarse_tiles):
            first = (j * coarse_tiles + n) * local
            rows = moved[first : first + local]
            slots[n * 4 + (j // 8) * 2, :, lanes] = rows[:, :128]
            slots[n * 4 + (j // 8) * 2 + 1, :, lanes] = rows[:, 128:]

    finish(table_copies)
    to_smem = pltpu.make_async_copy(table_all, table, local_sem.at[7])
    to_smem.start()
    to_smem.wait()
    homes = find_owners(table, n_tile, tiles, tuple(me_t * tiles + m for m in range(tiles)))
    owners = [slot_smem[0, t] // tiles for t in range(tiles)]
    for d in range(n_tile):
        chosen = jnp.int32(0)
        for m in range(tiles):
            chosen = jnp.where(homes[m] == d, m, chosen)
        cot_send[d] = slots[chosen]
    cot_recv[pl.ds(me_t, 1)] = cot_send[pl.ds(me_t, 1)]

    for k in range(1, n_outer):
        straight[k - 1].wait_recv()
        source = lax.rem(outer + n_outer - k, n_outer) * 2 + inner
        forwards.append(
            remote(
                rims.at[source],
                rims.at[source],
                rim_send.at[1, k],
                rim_recv.at[1, k],
                (across, me_c),
            )
        )
    cot_copies = to_tiles(1, lambda d: cot_send.at[d], cot_recv.at[me_t])

    finish(get_own)
    finish(small_copies)
    widen_weights(dot(cw_all[...].reshape(C, C * TAPS), tap_sel[...]), wide)
    down = jnp.zeros((C, 4 * C), F32)
    for c in range(n_chan):
        down = down + dot(dw_all[c], down_sel[c])
    down_t = down.T.astype(BF16)
    down = down.astype(BF16)

    def deinterleave(t):
        finish(feat_copies[t])
        pixels = feat_all[:, t].reshape(C, S * S)
        chunks = [pixels[:, 512 * j : 512 * j + 512] for j in range(8)]
        moved = dot(jnp.concatenate(chunks, axis=0), phase_sel[...])
        for j in range(8):
            rows = moved[j * C : (j + 1) * C]
            for p in range(4):
                phases[t, p, :, 128 * j : 128 * j + 128] = rows[:, p * 128 : p * 128 + 128]

    deinterleave(0)
    finish(forwards)
    for copy in straight:
        copy.wait_send()
    lane = lax.broadcasted_iota(jnp.int32, (local, 128), 1)
    for t in range(tiles):
        def half_of(link, rim):
            block = rims[link // tiles, lax.rem(link, tiles)].astype(F32)
            return jnp.where(rim >= 2, block[:, 128:], block[:, :128])

        strips = []
        corners = jnp.zeros((local, 128), F32)
        for k, place in enumerate((0, 0, 1, 1)):
            rim = lax.rem(k + 2 + et_smem[k, t], 4)
            held = half_of(el_smem[k, t], rim)
            strips.append(jnp.where(lax.rem(rim, 2) == place, held, pltpu.roll(held, S, 1)))
            link = cl_smem[k, t]
            rim = lax.rem(k + 3 + ct_smem[k, t], 4)
            held = half_of(jnp.maximum(link, 0), rim)
            near, far = held if k == 0 else pltpu.roll(held, k, 1), pltpu.roll(held, S + k, 1)
            value = jnp.where(lax.rem(rim, 2) == 0, near, far)
            value = jnp.where(link >= 0, value, jnp.zeros_like(value))
            corners = jnp.where(lane == k, value, corners)
        north, west, south, east = strips
        west_east = jnp.where(lane < S, west, east)
        north_south = jnp.where(lane < S, north, south)
        halos[t] = jnp.concatenate([west_east, north_south, corners], axis=1).astype(BF16)
    halo_all[pl.ds(me_c, 1)] = halos[pl.ds(me_c * per, per)][None]
    halo_copies = to_chans(4, lambda c: halos.at[pl.ds(c * per, per)], halo_all.at[me_c])

    finish(cot_copies)
    for t in range(tiles):
        cot_group[t] = cot_recv[owners[t]]
    cot_all[pl.ds(me_c, 1)] = cot_group[pl.ds(me_c * per, per)][None]
    cot_chan_copies = to_chans(
        6, lambda c: cot_group.at[pl.ds(c * per, per)], cot_all.at[me_c]
    )

    for t in range(1, per):
        deinterleave(t)
    finish(halo_copies)
    bias = jnp.concatenate([cb_all[...].reshape(C, 128)[:, :1]] * 4, axis=0)
    quarter_copies = []
    halo = jnp.concatenate([halo_all[:, t].reshape(C, 6 * S) for t in range(per)], axis=0)
    sides = dot(halo[:, : 2 * S], side_sel[...])
    caps = dot(halo[:, 2 * S :], cap_sel[...])
    for t in range(per):
        rows = slice(t * C, (t + 1) * C)
        fill_window([phases[t, p] for p in range(4)], sides[rows], caps[rows], window, t)
        pre = dot(wide[...], window[t]) + bias
        squashed = 1.0 / (1.0 + jnp.exp(-pre))
        slope[t] = squashed * (1.0 + pre * (1.0 - squashed))
        hidden[t] = (pre * squashed).astype(BF16)
        quarter[t] = dot(down, hidden[t]).astype(BF16)
        quarter_group[pl.ds(me_c, 1), t] = quarter[t, chan_rows(me_c)][None]
        quarter_copies += to_chans(
            FEAT + per + t, lambda c: quarter.at[t, chan_rows(c)], quarter_group.at[me_c, t]
        )

    finish(quarter_copies)
    for d in range(n_tile):
        chosen = jnp.int32(0)
        for t in range(tiles):
            chosen = jnp.where(owners[t] == d, t, chosen)
        quarter_send[d] = quarter_group[chosen // per, lax.rem(chosen, per)]
    quarter_recv[pl.ds(me_t, 1)] = quarter_send[pl.ds(me_t, 1)]
    quarter_copies = to_tiles(2, lambda d: quarter_send.at[d], quarter_recv.at[me_t])

    finish(cot_chan_copies)
    grad_wide = jnp.zeros((4 * C, 16 * C), F32)
    grad_down = jnp.zeros((C, 4 * C), F32)
    grad_bias = jnp.zeros((8, 4 * C), F32)
    ones = jnp.ones((8, QUARTER), BF16)
    for t in range(per):
        back = cot_all[:, t].reshape(C, QUARTER)
        grad_pre = (dot(down_t, back) * slope[t]).astype(BF16)
        grad_down = grad_down + dot_nt(back, hidden[t])
        grad_bias = grad_bias + dot_nt(ones, grad_pre)
        grad_wide = grad_wide + dot_nt(grad_pre, window[t])
    taps = []
    for dy in range(3):
        for dx in range(3):
            total = jnp.zeros((C, C), F32)
            for a in range(2):
                for b in range(2):
                    row = (a * 2 + b) * C
                    col = ((a + dy) * 4 + b + dx) * C
                    total = total + grad_wide[row : row + C, col : col + C]
            taps.append(total)
    pack[:, : TAPS * C] = split_dot_nt(jnp.concatenate(taps, axis=1), tap_sel[...])
    pack[:, TAPS * C :] = jnp.zeros((C, PACK - TAPS * C), F32)
    grad_down = split_dot_nt(grad_down, down_sel[...].reshape(4 * C, 4 * C))
    total = grad_bias[:1, :C]
    for ab in range(1, 4):
        total = total + grad_bias[:1, ab * C : ab * C + C]
    for c in range(n_chan):
        rows = slice(c * local, c * local + local)
        pack[c * local : c * local + 1, BIAS_COL : BIAS_COL + local] = total[:, rows]
        wide_cols = slice(c * 4 * local, (c + 1) * 4 * local)
        for n in range(C // local):
            col = DOWN_COL + n * 4 * local
            pack[rows, col : col + 4 * local] = grad_down[n * local : (n + 1) * local, wide_cols]

    pack_recv[pl.ds(me_c, 1)] = pack[chan_rows(me_c)][None]
    finish(to_chans(7, lambda c: pack.at[chan_rows(c)], pack_recv.at[me_c]))
    total = pack_recv[0]
    for c in range(1, n_chan):
        total = total + pack_recv[c]
    n_pieces = PACK // 128
    if n_tile == n_pieces:
        for n in range(n_pieces):
            pieces[n] = total[:, n * 128 : n * 128 + 128]
        pieces_recv[pl.ds(me_t, 1)] = pieces[pl.ds(me_t, 1)]
        finish(to_tiles(3, lambda d: pieces.at[d], pieces_recv.at[me_t]))
        total = pieces_recv[0]
        for s in range(1, n_tile):
            total = total + pieces_recv[s]
        grads_out[pl.ds(me_t, 1)] = total[None]
        finish(to_tiles(4, lambda d: grads_out.at[me_t], grads_out.at[me_t]))
    else:
        pieces[pl.ds(me_t, 1)] = total[None]
        finish(to_tiles(3, lambda d: pieces.at[me_t], pieces.at[me_t]))
        total = pieces[0]
        for s in range(1, n_tile):
            total = total + pieces[s]
        for n in range(n_pieces):
            grads_out[n] = total[:, n * 128 : n * 128 + 128]

    finish(quarter_copies)
    for m in range(tiles):
        placed_out[m] = quarter_recv[homes[m]]


def finish_kernel(placed, grads, join_sel, coarse, grad_conv, grad_bias, grad_down):
    local = coarse.shape[1]
    chunks = []
    for n in range(coarse.shape[0]):
        for j in range(16):
            lanes = slice((j % 8) * 128, (j % 8) * 128 + 128)
            q = n * 4 + (j // 8) * 2
            chunks.append(jnp.concatenate([placed[q, :, lanes], placed[q + 1, :, lanes]], axis=1))
    moved = dot(jnp.concatenate(chunks, axis=0), join_sel[...]).astype(BF16)
    for n in range(coarse.shape[0]):
        for j in range(16):
            first = (n * 16 + j) * local
            coarse[n, :, 256 * j : 256 * j + 256] = moved[first : first + local]
    whole = jnp.concatenate([grads[n] for n in range(grads.shape[0])], axis=1)
    grad_conv[...] = whole[:, : TAPS * C]
    grad_bias[...] = whole[:1, BIAS_COL : BIAS_COL + local]
    for n in range(C // local):
        col = DOWN_COL + n * 4 * local
        grad_down[n * local : (n + 1) * local] = whole[:, col : col + 4 * local]


def on_device(
    n_tile,
    n_chan,
    features,
    conv_weight,
    conv_bias,
    down_weight,
    cotangent,
    edge_links,
    edge_turns,
    corner_links,
    corner_turns,
    child_slot,
):
    tiles, local = features.shape[0], features.shape[1]
    per = tiles // n_chan
    n_pieces = PACK // 128
    hbm = pl.BlockSpec(memory_space=pltpu.HBM)
    vmem = pl.BlockSpec(memory_space=pltpu.VMEM)
    smem = pl.BlockSpec(memory_space=pltpu.SMEM)
    tables = [edge_links.T, edge_turns.T, corner_links.T, corner_turns.T, child_slot[None]]

    def const(values):
        return jnp.asarray(values, BF16)

    half = half_selector()
    selectors = [
        const(rim_selector()),
        const(half),
        const(phase_selector()),
        const(side_selector()),
        const(cap_selector()),
        const(tap_selector()),
        const(down_selector(n_chan)),
    ]
    split = n_tile == n_pieces
    piece_shape = (n_tile, local, 128 if split else PACK)
    dma = pltpu.SemaphoreType.DMA
    placed, grads = pl.pallas_call(
        functools.partial(level_kernel, n_tile, n_chan, tiles),
        out_shape=[
            jax.ShapeDtypeStruct((tiles, local, QUARTER), BF16),
            jax.ShapeDtypeStruct((n_pieces, local, 128), F32),
        ],
        in_specs=[hbm] * 11 + [smem] * 6,
        out_specs=[vmem] * 2,
        scratch_shapes=[
            pltpu.VMEM(features.shape, BF16),
            pltpu.VMEM(cotangent.shape, BF16),
        ]
        + [pltpu.VMEM(selector.shape, BF16) for selector in selectors]
        + [
            pltpu.VMEM((n_chan, per, local, S * S), BF16),
            pltpu.VMEM((n_chan, local, C * TAPS), BF16),
            pltpu.VMEM((n_chan, C, local * 4), BF16),
            pltpu.VMEM((n_chan, local, 128), F32),
            pltpu.VMEM((n_tile, tiles, 128), jnp.int32),
            pltpu.SMEM((n_tile, tiles, 128), jnp.int32),
            pltpu.VMEM((n_tile, tiles, local, 4 * S), BF16),
            pltpu.VMEM((tiles, local, 6 * S), BF16),
            pltpu.VMEM((n_chan, per, local, 6 * S), BF16),
            pltpu.VMEM((tiles, local, QUARTER), BF16),
            pltpu.VMEM((n_tile, local, QUARTER), BF16),
            pltpu.VMEM((n_tile, local, QUARTER), BF16),
            pltpu.VMEM((tiles, local, QUARTER), BF16),
            pltpu.VMEM((n_chan, per, local, QUARTER), BF16),
            pltpu.VMEM((4 * C, 16 * C), BF16),
            pltpu.VMEM((per, 4, C, QUARTER), F32),
            pltpu.VMEM((per, 16 * C, QUARTER), BF16),
            pltpu.VMEM((per, 4 * C, QUARTER), F32),
            pltpu.VMEM((per, 4 * C, QUARTER), BF16),
            pltpu.VMEM((per, C, QUARTER), BF16),
            pltpu.VMEM((n_chan, per, local, QUARTER), BF16),
            pltpu.VMEM((n_tile, local, QUARTER), BF16),
            pltpu.VMEM((n_tile, local, QUARTER), BF16),
            pltpu.VMEM((C, PACK), F32),
            pltpu.VMEM((n_chan, local, PACK), F32),
            pltpu.VMEM(piece_shape, F32),
            pltpu.VMEM((n_tile, local, 128), F32),
            dma((13,)),
            dma((FEAT + 2 * per, n_chan)),
            dma((FEAT + 2 * per, n_chan)),
            dma((5, n_tile)),
            dma((5, n_tile)),
            dma((2, n_tile // 2)),
            dma((2, n_tile // 2)),
        ],
        compiler_params=pltpu.CompilerParams(
            collective_id=0, has_side_effects=True, vmem_limit_bytes=VMEM_LIMIT
        ),
        name="unet_level",
    )(features, cotangent, conv_weight, down_weight, *selectors, conv_bias, *tables)
    coarse, grad_conv, grad_bias, grad_down = pl.pallas_call(
        finish_kernel,
        out_shape=[
            jax.ShapeDtypeStruct(cotangent.shape, BF16),
            jax.ShapeDtypeStruct(conv_weight.shape, F32),
            jax.ShapeDtypeStruct((1, local), F32),
            jax.ShapeDtypeStruct(down_weight.shape, F32),
        ],
        in_specs=[vmem] * 3,
        out_specs=[vmem] * 4,
        compiler_params=pltpu.CompilerParams(vmem_limit_bytes=VMEM_LIMIT),
        name="finish",
    )(placed, grads, const(half.T))
    return (coarse, grad_conv, grad_bias.reshape(local), grad_down)


def solution(mesh):
    n_tile, n_chan = mesh.shape["tile"], mesh.shape["chan"]
    in_specs = (
        P("tile", "chan", None),
        P("chan", None),
        P("chan"),
        P(None, "chan"),
        P("tile", "chan", None),
        P("tile", None),
        P("tile", None),
        P("tile", None),
        P("tile", None),
        P("tile"),
    )
    out_specs = (P("tile", "chan", None), P("chan", None), P("chan"), P(None, "chan"))
    return jax.shard_map(
        functools.partial(on_device, n_tile, n_chan),
        mesh=mesh,
        in_specs=in_specs,
        out_specs=out_specs,
        check_vma=False,
    )
```

```python
import functools

import jax
import jax.numpy as jnp
import numpy as np
from jax import lax
from jax.experimental import pallas as pl
from jax.experimental.pallas import tpu as pltpu
from jax.sharding import PartitionSpec as P

C = 64
S = 64
H = S // 2
QUARTER = H * H
TAPS = 9
MESH = pl.DeviceIdType.MESH
F32 = jnp.float32
BF16 = jnp.bfloat16
VMEM_LIMIT = 63 * 1024 * 1024
PACK = 1024
FEAT = 8
BIAS_COL = TAPS * C
DOWN_COL = BIAS_COL + C


def rim_selector():
    pick = np.zeros((S * S, 4 * S), np.float32)
    for n in range(S):
        pick[S - 1 - n, n] = 1
        pick[n * S, S + n] = 1
        pick[(S - 1) * S + n, 2 * S + n] = 1
        pick[(S - 1 - n) * S + S - 1, 3 * S + n] = 1
    return pick


def phase_selector():
    lane = np.arange(8 * S)
    row, col = lane // S, lane % S
    target = ((row % 2) * 2 + col % 2) * 128 + (row // 2) * H + col // 2
    pick = np.zeros((8 * S, 8 * S), np.float32)
    pick[lane, target] = 1
    return pick


def half_selector():
    lane = np.arange(4 * S)
    row, col = lane // S, lane % S
    pick = np.zeros((4 * S, 4 * S), np.float32)
    pick[lane, (col // H) * 128 + row * H + col % H] = 1
    return pick


def side_selector():
    pick = np.zeros((2 * S, 4 * QUARTER), np.float32)
    for a in range(2):
        for u in range(H):
            pick[S - 1 - (2 * u + a), a * QUARTER + u * H] = 1
            pick[S + 2 * u + a, (2 + a) * QUARTER + u * H + H - 1] = 1
    return pick


def cap_selector():
    pick = np.zeros((4 * S, 8 * 128), np.float32)
    for wx in range(4):
        for v in range(H):
            x = 2 * v + wx - 1
            top = 128 + 0 if x < 0 else 128 + 3 if x >= S else x
            low = 128 + 1 if x < 0 else 128 + 2 if x >= S else S + S - 1 - x
            pick[top, wx * 128 + v] = 1
            pick[low, (4 + wx) * 128 + 96 + v] = 1
    return pick


def tap_selector():
    pick = np.zeros((C * TAPS, C * TAPS), np.float32)
    for i in range(C):
        for tap in range(TAPS):
            pick[i * TAPS + tap, tap * C + i] = 1
    return pick


def down_selector(n_chan):
    local = C // n_chan
    pick = np.zeros((n_chan, local * 4, C * 4), np.float32)
    for i in range(C):
        for ab in range(4):
            pick[i // local, (i % local) * 4 + ab, ab * C + i] = 1
    return pick


def dot(a, b):
    return jnp.dot(a, b, preferred_element_type=F32)


def dot_nt(a, b):
    return lax.dot_general(a, b, (((1,), (1,)), ((), ())), preferred_element_type=F32)


def split_dot_nt(a, selector):
    high = a.astype(BF16)
    rest = a - high.astype(F32)
    middle = rest.astype(BF16)
    low = (rest - middle.astype(F32)).astype(BF16)
    rows = a.shape[0]
    moved = dot_nt(jnp.concatenate([high, middle, low], axis=0), selector)
    return moved[:rows] + moved[rows : 2 * rows] + moved[2 * rows :]


def greet(n_tile, n_chan, me_t, me_c):
    barrier = pltpu.get_barrier_semaphore()
    for k in range(1, n_tile):
        peer = lax.rem(me_t + k, n_tile)
        pl.semaphore_signal(barrier, inc=1, device_id=(peer, me_c), device_id_type=MESH)
    for k in range(1, n_chan):
        peer = lax.rem(me_c + k, n_chan)
        pl.semaphore_signal(barrier, inc=1, device_id=(me_t, peer), device_id_type=MESH)


def remote(src, dst, send_sem, recv_sem, device):
    copy = pltpu.make_async_remote_copy(
        src_ref=src,
        dst_ref=dst,
        send_sem=send_sem,
        recv_sem=recv_sem,
        device_id=device,
        device_id_type=MESH,
    )
    copy.start()
    return copy


def find_owners(table, groups, tiles, wanted):
    def step(s, found):
        for t in range(tiles):
            value = table[s, t, 0]
            found = tuple(jnp.where(value == w, s, f) for w, f in zip(wanted, found))
        return found

    return lax.fori_loop(0, groups, step, (jnp.int32(0),) * len(wanted))


def widen_weights(taps, wide):
    none = jnp.zeros((C, C), F32)
    for a in range(2):
        for b in range(2):
            pieces = []
            for wy in range(4):
                for wx in range(4):
                    dy, dx = wy - a, wx - b
                    if 0 <= dy < 3 and 0 <= dx < 3:
                        tap = 3 * dy + dx
                        pieces.append(taps[:, tap * C : tap * C + C])
                    else:
                        pieces.append(none)
            row = (a * 2 + b) * C
            wide[row : row + C, :] = jnp.concatenate(pieces, axis=1).astype(BF16)


def fill_window(phase, sides, caps, window, t):
    lane = lax.broadcasted_iota(jnp.int32, (C, QUARTER), 1)
    first_col = lax.rem(lane, H) == 0
    last_col = lax.rem(lane, H) == H - 1
    lane_cap = lax.broadcasted_iota(jnp.int32, (C, 128), 1)
    for a in range(2):
        even, odd = phase[a * 2], phase[a * 2 + 1]
        west = jnp.where(
            first_col, sides[:, a * QUARTER : (a + 1) * QUARTER], pltpu.roll(odd, 1, 1)
        )
        east = jnp.where(
            last_col,
            sides[:, (2 + a) * QUARTER : (3 + a) * QUARTER],
            pltpu.roll(even, QUARTER - 1, 1),
        )
        for wx, middle in enumerate((west, even, odd, east)):
            row = ((1 + a) * 4 + wx) * C
            window[t, row : row + C, :] = middle.astype(BF16)
            if a == 1:
                moved = pltpu.roll(middle, H, 1)
                cap = caps[:, wx * 128 : wx * 128 + 128]
                head = jnp.where(lane_cap < H, cap, moved[:, :128])
                moved = jnp.concatenate([head, moved[:, 128:]], axis=1)
                row = wx * C
            else:
                moved = pltpu.roll(middle, QUARTER - H, 1)
                cap = caps[:, (4 + wx) * 128 : (5 + wx) * 128]
                tail = jnp.where(lane_cap >= 128 - H, cap, moved[:, QUARTER - 128 :])
                moved = jnp.concatenate([moved[:, : QUARTER - 128], tail], axis=1)
                row = (12 + wx) * C
            window[t, row : row + C, :] = moved.astype(BF16)


def level_kernel(
    n_tile,
    n_chan,
    tiles,
    feat_hbm,
    cot_hbm,
    cw_hbm,
    dw_hbm,
    rim_sel_hbm,
    half_sel_hbm,
    phase_sel_hbm,
    side_sel_hbm,
    cap_sel_hbm,
    tap_sel_hbm,
    down_sel_hbm,
    cb_smem,
    el_smem,
    et_smem,
    cl_smem,
    ct_smem,
    slot_smem,
    coarse_out,
    grads_out,
    feat,
    cot,
    rim_sel,
    half_sel,
    phase_sel,
    side_sel,
    cap_sel,
    tap_sel,
    down_sel,
    feat_all,
    cw_all,
    dw_all,
    cb_all,
    table_all,
    table,
    rims,
    halos,
    halo_all,
    slots,
    cot_send,
    cot_recv,
    cot_group,
    cot_all,
    wide,
    phases,
    window,
    slope,
    hidden,
    quarter,
    quarter_group,
    quarter_send,
    quarter_recv,
    pack,
    pack_recv,
    pieces,
    pieces_recv,
    local_sem,
    chan_send,
    chan_recv,
    tile_send,
    tile_recv,
    rim_send,
    rim_recv,
):
    me_t = lax.axis_index("tile")
    me_c = lax.axis_index("chan")
    per = tiles // n_chan
    local = feat.shape[1]
    n_outer = n_tile // 2
    outer, inner = me_t // 2, lax.rem(me_t, 2)

    greet(n_tile, n_chan, me_t, me_c)

    def fetch(src, dst, k):
        copy = pltpu.make_async_copy(src, dst, local_sem.at[k])
        copy.start()
        return copy

    get_feat = fetch(feat_hbm, feat, 0)
    get_rim_sel = fetch(rim_sel_hbm, rim_sel, 1)
    get_cot = fetch(cot_hbm, cot, 2)
    get_half_sel = fetch(half_sel_hbm, half_sel, 3)
    get_own = [
        fetch(cw_hbm, cw_all.at[me_c], 5),
        fetch(dw_hbm, dw_all.at[me_c], 6),
        fetch(feat_hbm.at[pl.ds(me_c * per, per)], feat_all.at[me_c], 4),
        fetch(phase_sel_hbm, phase_sel, 8),
        fetch(side_sel_hbm, side_sel, 9),
        fetch(cap_sel_hbm, cap_sel, 10),
        fetch(tap_sel_hbm, tap_sel, 11),
        fetch(down_sel_hbm, down_sel, 12),
    ]
    row = lax.broadcasted_iota(jnp.int32, (local, 128), 0)
    bias = jnp.zeros((local, 128), F32)
    for n in range(local):
        bias = jnp.where(row == n, cb_smem[n], bias)
    cb_all[pl.ds(me_c, 1)] = bias[None]
    row = lax.broadcasted_iota(jnp.int32, (tiles, 128), 0)
    own_slots = jnp.zeros((tiles, 128), jnp.int32)
    for t in range(tiles):
        own_slots = jnp.where(row == t, slot_smem[0, t], own_slots)
    table_all[pl.ds(me_t, 1)] = own_slots[None]

    pl.semaphore_wait(pltpu.get_barrier_semaphore(), n_tile - 1 + n_chan - 1)

    def to_tiles(kind, src, dst):
        copies = []
        for k in range(1, n_tile):
            d = lax.rem(me_t + k, n_tile)
            copies.append(
                remote(
                    src(d), dst, tile_send.at[kind, k], tile_recv.at[kind, k], (d, me_c)
                )
            )
        return copies

    def to_chans(kind, src, dst):
        copies = []
        for k in range(1, n_chan):
            c = lax.rem(me_c + k, n_chan)
            copies.append(
                remote(
                    src(c), dst, chan_send.at[kind, k], chan_recv.at[kind, k], (me_t, c)
                )
            )
        return copies

    def finish(copies):
        for copy in copies:
            copy.wait()

    def chan_rows(c):
        return pl.ds(pl.multiple_of(c * local, local), local)

    table_copies = to_tiles(0, lambda d: table_all.at[me_t], table_all.at[me_t])
    small_copies = (
        to_chans(1, lambda c: cw_hbm, cw_all.at[me_c])
        + to_chans(2, lambda c: dw_hbm, dw_all.at[me_c])
        + to_chans(3, lambda c: cb_all.at[me_c], cb_all.at[me_c])
    )
    feat_copies = [
        to_chans(FEAT + t, lambda c: feat_hbm.at[c * per + t], feat_all.at[me_c, t])
        for t in range(per)
    ]

    get_feat.wait()
    get_rim_sel.wait()
    pixels = feat[...].reshape(tiles * local, S * S)
    my_rims = dot(pixels, rim_sel[...]).astype(BF16)
    rims[pl.ds(me_t, 1)] = my_rims.reshape(1, tiles, local, 4 * S)
    across = outer * 2 + 1 - inner
    forwards = [
        remote(
            rims.at[me_t], rims.at[me_t], rim_send.at[1, 0], rim_recv.at[1, 0], (across, me_c)
        )
    ]
    straight = []
    for k in range(1, n_outer):
        d = lax.rem(outer + k, n_outer) * 2 + inner
        straight.append(
            remote(rims.at[me_t], rims.at[me_t], rim_send.at[0, k], rim_recv.at[0, k], (d, me_c))
        )

    get_cot.wait()
    get_half_sel.wait()
    coarse_tiles = cot.shape[0]
    cots = cot[...].reshape(coarse_tiles * local, S * S)
    chunks = [cots[:, 256 * j : 256 * j + 256] for j in range(16)]
    moved = dot(jnp.concatenate(chunks, axis=0), half_sel[...]).astype(BF16)
    for j in range(16):
        lanes = slice((j % 8) * 128, (j % 8) * 128 + 128)
        for n in range(coarse_tiles):
            first = (j * coarse_tiles + n) * local
            rows = moved[first : first + local]
            slots[n * 4 + (j // 8) * 2, :, lanes] = rows[:, :128]
            slots[n * 4 + (j // 8) * 2 + 1, :, lanes] = rows[:, 128:]

    finish(table_copies)
    to_smem = pltpu.make_async_copy(table_all, table, local_sem.at[7])
    to_smem.start()
    to_smem.wait()
    homes = find_owners(table, n_tile, tiles, tuple(me_t * tiles + m for m in range(tiles)))
    owners = [slot_smem[0, t] // tiles for t in range(tiles)]
    for d in range(n_tile):
        chosen = jnp.int32(0)
        for m in range(tiles):
            chosen = jnp.where(homes[m] == d, m, chosen)
        cot_send[d] = slots[chosen]
    cot_recv[pl.ds(me_t, 1)] = cot_send[pl.ds(me_t, 1)]

    for k in range(1, n_outer):
        straight[k - 1].wait_recv()
        source = lax.rem(outer + n_outer - k, n_outer) * 2 + inner
        forwards.append(
            remote(
                rims.at[source],
                rims.at[source],
                rim_send.at[1, k],
                rim_recv.at[1, k],
                (across, me_c),
            )
        )
    cot_copies = to_tiles(1, lambda d: cot_send.at[d], cot_recv.at[me_t])

    finish(get_own)
    finish(small_copies)
    widen_weights(dot(cw_all[...].reshape(C, C * TAPS), tap_sel[...]), wide)
    down = jnp.zeros((C, 4 * C), F32)
    for c in range(n_chan):
        down = down + dot(dw_all[c], down_sel[c])
    down_t = down.T.astype(BF16)
    down = down.astype(BF16)

    def deinterleave(t):
        finish(feat_copies[t])
        pixels = feat_all[:, t].reshape(C, S * S)
        chunks = [pixels[:, 512 * j : 512 * j + 512] for j in range(8)]
        moved = dot(jnp.concatenate(chunks, axis=0), phase_sel[...])
        for j in range(8):
            rows = moved[j * C : (j + 1) * C]
            for p in range(4):
                phases[t, p, :, 128 * j : 128 * j + 128] = rows[:, p * 128 : p * 128 + 128]

    deinterleave(0)
    finish(forwards)
    for copy in straight:
        copy.wait_send()
    lane = lax.broadcasted_iota(jnp.int32, (local, 128), 1)
    for t in range(tiles):
        def half_of(link, rim):
            block = rims[link // tiles, lax.rem(link, tiles)].astype(F32)
            return jnp.where(rim >= 2, block[:, 128:], block[:, :128])

        strips = []
        corners = jnp.zeros((local, 128), F32)
        for k, place in enumerate((0, 0, 1, 1)):
            rim = lax.rem(k + 2 + et_smem[k, t], 4)
            held = half_of(el_smem[k, t], rim)
            strips.append(jnp.where(lax.rem(rim, 2) == place, held, pltpu.roll(held, S, 1)))
            link = cl_smem[k, t]
            rim = lax.rem(k + 3 + ct_smem[k, t], 4)
            held = half_of(jnp.maximum(link, 0), rim)
            near, far = held if k == 0 else pltpu.roll(held, k, 1), pltpu.roll(held, S + k, 1)
            value = jnp.where(lax.rem(rim, 2) == 0, near, far)
            value = jnp.where(link >= 0, value, jnp.zeros_like(value))
            corners = jnp.where(lane == k, value, corners)
        north, west, south, east = strips
        west_east = jnp.where(lane < S, west, east)
        north_south = jnp.where(lane < S, north, south)
        halos[t] = jnp.concatenate([west_east, north_south, corners], axis=1).astype(BF16)
    halo_all[pl.ds(me_c, 1)] = halos[pl.ds(me_c * per, per)][None]
    halo_copies = to_chans(4, lambda c: halos.at[pl.ds(c * per, per)], halo_all.at[me_c])

    for t in range(1, per):
        deinterleave(t)
    finish(halo_copies)
    bias = jnp.concatenate([cb_all[...].reshape(C, 128)[:, :1]] * 4, axis=0)
    def forward_cotangent():
        finish(cot_copies)
        for t in range(tiles):
            cot_group[t] = cot_recv[owners[t]]
        cot_all[pl.ds(me_c, 1)] = cot_group[pl.ds(me_c * per, per)][None]
        return to_chans(
            6, lambda c: cot_group.at[pl.ds(c * per, per)], cot_all.at[me_c]
        )

    quarter_copies = []
    halo = jnp.concatenate([halo_all[:, t].reshape(C, 6 * S) for t in range(per)], axis=0)
    sides = dot(halo[:, : 2 * S], side_sel[...])
    caps = dot(halo[:, 2 * S :], cap_sel[...])
    for t in range(per):
        rows = slice(t * C, (t + 1) * C)
        fill_window([phases[t, p] for p in range(4)], sides[rows], caps[rows], window, t)
        pre = dot(wide[...], window[t]) + bias
        squashed = 1.0 / (1.0 + jnp.exp(-pre))
        slope[t] = squashed * (1.0 + pre * (1.0 - squashed))
        hidden[t] = (pre * squashed).astype(BF16)
        quarter[t] = dot(down, hidden[t]).astype(BF16)
        quarter_group[pl.ds(me_c, 1), t] = quarter[t, chan_rows(me_c)][None]
        quarter_copies += to_chans(
            FEAT + per + t, lambda c: quarter.at[t, chan_rows(c)], quarter_group.at[me_c, t]
        )
        if t == 0:
            cot_chan_copies = forward_cotangent()

    def forward_quarters():
        finish(quarter_copies)
        for d in range(n_tile):
            chosen = jnp.int32(0)
            for t in range(tiles):
                chosen = jnp.where(owners[t] == d, t, chosen)
            quarter_send[d] = quarter_group[chosen // per, lax.rem(chosen, per)]
        quarter_recv[pl.ds(me_t, 1)] = quarter_send[pl.ds(me_t, 1)]
        return to_tiles(2, lambda d: quarter_send.at[d], quarter_recv.at[me_t])

    finish(cot_chan_copies)
    grad_wide = jnp.zeros((4 * C, 16 * C), F32)
    grad_down = jnp.zeros((C, 4 * C), F32)
    grad_bias = jnp.zeros((8, 4 * C), F32)
    ones = jnp.ones((8, QUARTER), BF16)
    for t in range(per):
        back = cot_all[:, t].reshape(C, QUARTER)
        grad_pre = (dot(down_t, back) * slope[t]).astype(BF16)
        grad_down = grad_down + dot_nt(back, hidden[t])
        grad_bias = grad_bias + dot_nt(ones, grad_pre)
        grad_wide = grad_wide + dot_nt(grad_pre, window[t])
        if t == 0:
            quarter_moves = forward_quarters()
    taps = []
    for dy in range(3):
        for dx in range(3):
            total = jnp.zeros((C, C), F32)
            for a in range(2):
                for b in range(2):
                    row = (a * 2 + b) * C
                    col = ((a + dy) * 4 + b + dx) * C
                    total = total + grad_wide[row : row + C, col : col + C]
            taps.append(total)
    pack[:, : TAPS * C] = split_dot_nt(jnp.concatenate(taps, axis=1), tap_sel[...])
    pack[:, TAPS * C :] = jnp.zeros((C, PACK - TAPS * C), F32)
    grad_down = split_dot_nt(grad_down, down_sel[...].reshape(4 * C, 4 * C))
    total = grad_bias[:1, :C]
    for ab in range(1, 4):
        total = total + grad_bias[:1, ab * C : ab * C + C]
    for c in range(n_chan):
        rows = slice(c * local, c * local + local)
        pack[c * local : c * local + 1, BIAS_COL : BIAS_COL + local] = total[:, rows]
        wide_cols = slice(c * 4 * local, (c + 1) * 4 * local)
        for n in range(C // local):
            col = DOWN_COL + n * 4 * local
            pack[rows, col : col + 4 * local] = grad_down[n * local : (n + 1) * local, wide_cols]

    def join_quarters():
        finish(quarter_moves)
        placed = [quarter_recv[home] for home in homes]
        chunks = []
        for n in range(coarse_tiles):
            for j in range(16):
                lanes = slice((j % 8) * 128, (j % 8) * 128 + 128)
                q = n * 4 + (j // 8) * 2
                chunks.append(jnp.concatenate([placed[q][:, lanes], placed[q + 1][:, lanes]], 1))
        moved = dot_nt(jnp.concatenate(chunks, axis=0), half_sel[...]).astype(BF16)
        for n in range(coarse_tiles):
            for j in range(16):
                first = (n * 16 + j) * local
                coarse_out[n, :, 256 * j : 256 * j + 256] = moved[first : first + local]

    pack_recv[pl.ds(me_c, 1)] = pack[chan_rows(me_c)][None]
    finish(to_chans(7, lambda c: pack.at[chan_rows(c)], pack_recv.at[me_c]))
    total = pack_recv[0]
    for c in range(1, n_chan):
        total = total + pack_recv[c]
    n_pieces = PACK // 128
    if n_tile == n_pieces:
        for n in range(n_pieces):
            pieces[n] = total[:, n * 128 : n * 128 + 128]
        pieces_recv[pl.ds(me_t, 1)] = pieces[pl.ds(me_t, 1)]
        piece_copies = to_tiles(3, lambda d: pieces.at[d], pieces_recv.at[me_t])
        join_quarters()
        finish(piece_copies)
        total = pieces_recv[0]
        for s in range(1, n_tile):
            total = total + pieces_recv[s]
        grads_out[pl.ds(me_t, 1)] = total[None]
        finish(to_tiles(4, lambda d: grads_out.at[me_t], grads_out.at[me_t]))
    else:
        pieces[pl.ds(me_t, 1)] = total[None]
        piece_copies = to_tiles(3, lambda d: pieces.at[me_t], pieces.at[me_t])
        join_quarters()
        finish(piece_copies)
        total = pieces[0]
        for s in range(1, n_tile):
            total = total + pieces[s]
        for n in range(n_pieces):
            grads_out[n] = total[:, n * 128 : n * 128 + 128]


def finish_kernel(joined, grads, coarse, grad_conv, grad_bias, grad_down):
    local = coarse.shape[1]
    coarse[...] = joined[...]
    whole = jnp.concatenate([grads[n] for n in range(grads.shape[0])], axis=1)
    grad_conv[...] = whole[:, : TAPS * C]
    grad_bias[...] = whole[:1, BIAS_COL : BIAS_COL + local]
    for n in range(C // local):
        col = DOWN_COL + n * 4 * local
        grad_down[n * local : (n + 1) * local] = whole[:, col : col + 4 * local]


def on_device(
    n_tile,
    n_chan,
    features,
    conv_weight,
    conv_bias,
    down_weight,
    cotangent,
    edge_links,
    edge_turns,
    corner_links,
    corner_turns,
    child_slot,
):
    tiles, local = features.shape[0], features.shape[1]
    per = tiles // n_chan
    n_pieces = PACK // 128
    hbm = pl.BlockSpec(memory_space=pltpu.HBM)
    vmem = pl.BlockSpec(memory_space=pltpu.VMEM)
    smem = pl.BlockSpec(memory_space=pltpu.SMEM)
    tables = [edge_links.T, edge_turns.T, corner_links.T, corner_turns.T, child_slot[None]]

    def const(values):
        return jnp.asarray(values, BF16)

    half = half_selector()
    selectors = [
        const(rim_selector()),
        const(half),
        const(phase_selector()),
        const(side_selector()),
        const(cap_selector()),
        const(tap_selector()),
        const(down_selector(n_chan)),
    ]
    split = n_tile == n_pieces
    piece_shape = (n_tile, local, 128 if split else PACK)
    dma = pltpu.SemaphoreType.DMA
    joined, grads = pl.pallas_call(
        functools.partial(level_kernel, n_tile, n_chan, tiles),
        out_shape=[
            jax.ShapeDtypeStruct(cotangent.shape, BF16),
            jax.ShapeDtypeStruct((n_pieces, local, 128), F32),
        ],
        in_specs=[hbm] * 11 + [smem] * 6,
        out_specs=[vmem] * 2,
        scratch_shapes=[
            pltpu.VMEM(features.shape, BF16),
            pltpu.VMEM(cotangent.shape, BF16),
        ]
        + [pltpu.VMEM(selector.shape, BF16) for selector in selectors]
        + [
            pltpu.VMEM((n_chan, per, local, S * S), BF16),
            pltpu.VMEM((n_chan, local, C * TAPS), BF16),
            pltpu.VMEM((n_chan, C, local * 4), BF16),
            pltpu.VMEM((n_chan, local, 128), F32),
            pltpu.VMEM((n_tile, tiles, 128), jnp.int32),
            pltpu.SMEM((n_tile, tiles, 128), jnp.int32),
            pltpu.VMEM((n_tile, tiles, local, 4 * S), BF16),
            pltpu.VMEM((tiles, local, 6 * S), BF16),
            pltpu.VMEM((n_chan, per, local, 6 * S), BF16),
            pltpu.VMEM((tiles, local, QUARTER), BF16),
            pltpu.VMEM((n_tile, local, QUARTER), BF16),
            pltpu.VMEM((n_tile, local, QUARTER), BF16),
            pltpu.VMEM((tiles, local, QUARTER), BF16),
            pltpu.VMEM((n_chan, per, local, QUARTER), BF16),
            pltpu.VMEM((4 * C, 16 * C), BF16),
            pltpu.VMEM((per, 4, C, QUARTER), F32),
            pltpu.VMEM((per, 16 * C, QUARTER), BF16),
            pltpu.VMEM((per, 4 * C, QUARTER), F32),
            pltpu.VMEM((per, 4 * C, QUARTER), BF16),
            pltpu.VMEM((per, C, QUARTER), BF16),
            pltpu.VMEM((n_chan, per, local, QUARTER), BF16),
            pltpu.VMEM((n_tile, local, QUARTER), BF16),
            pltpu.VMEM((n_tile, local, QUARTER), BF16),
            pltpu.VMEM((C, PACK), F32),
            pltpu.VMEM((n_chan, local, PACK), F32),
            pltpu.VMEM(piece_shape, F32),
            pltpu.VMEM((n_tile, local, 128), F32),
            dma((13,)),
            dma((FEAT + 2 * per, n_chan)),
            dma((FEAT + 2 * per, n_chan)),
            dma((5, n_tile)),
            dma((5, n_tile)),
            dma((2, n_tile // 2)),
            dma((2, n_tile // 2)),
        ],
        compiler_params=pltpu.CompilerParams(
            collective_id=0, has_side_effects=True, vmem_limit_bytes=VMEM_LIMIT
        ),
        name="unet_level",
    )(features, cotangent, conv_weight, down_weight, *selectors, conv_bias, *tables)
    coarse, grad_conv, grad_bias, grad_down = pl.pallas_call(
        finish_kernel,
        out_shape=[
            jax.ShapeDtypeStruct(cotangent.shape, BF16),
            jax.ShapeDtypeStruct(conv_weight.shape, F32),
            jax.ShapeDtypeStruct((1, local), F32),
            jax.ShapeDtypeStruct(down_weight.shape, F32),
        ],
        in_specs=[vmem] * 2,
        out_specs=[vmem] * 4,
        compiler_params=pltpu.CompilerParams(vmem_limit_bytes=VMEM_LIMIT),
        name="finish",
    )(joined, grads)
    return (coarse, grad_conv, grad_bias.reshape(local), grad_down)


def solution(mesh):
    n_tile, n_chan = mesh.shape["tile"], mesh.shape["chan"]
    in_specs = (
        P("tile", "chan", None),
        P("chan", None),
        P("chan"),
        P(None, "chan"),
        P("tile", "chan", None),
        P("tile", None),
        P("tile", None),
        P("tile", None),
        P("tile", None),
        P("tile"),
    )
    out_specs = (P("tile", "chan", None), P("chan", None), P("chan"), P(None, "chan"))
    return jax.shard_map(
        functools.partial(on_device, n_tile, n_chan),
        mesh=mesh,
        in_specs=in_specs,
        out_specs=out_specs,
        check_vma=False,
    )
```

```python
import functools

import jax
import jax.numpy as jnp
import numpy as np
from jax import lax
from jax.experimental import pallas as pl
from jax.experimental.pallas import tpu as pltpu
from jax.sharding import PartitionSpec as P

C = 64
S = 64
H = S // 2
QUARTER = H * H
TAPS = 9
MESH = pl.DeviceIdType.MESH
F32 = jnp.float32
BF16 = jnp.bfloat16
VMEM_LIMIT = 63 * 1024 * 1024
PACK = 1024
PACK_USED = 896
FEAT = 8
BIAS_COL = TAPS * C
DOWN_COL = BIAS_COL + C


def rim_selector():
    pick = np.zeros((S * S, 4 * S), np.float32)
    for n in range(S):
        pick[S - 1 - n, n] = 1
        pick[n * S, S + n] = 1
        pick[(S - 1) * S + n, 2 * S + n] = 1
        pick[(S - 1 - n) * S + S - 1, 3 * S + n] = 1
    return pick


def phase_selector():
    lane = np.arange(8 * S)
    row, col = lane // S, lane % S
    target = ((row % 2) * 2 + col % 2) * 128 + (row // 2) * H + col // 2
    pick = np.zeros((8 * S, 8 * S), np.float32)
    pick[lane, target] = 1
    return pick


def half_selector():
    lane = np.arange(4 * S)
    row, col = lane // S, lane % S
    pick = np.zeros((4 * S, 4 * S), np.float32)
    pick[lane, (col // H) * 128 + row * H + col % H] = 1
    return pick


def side_selector():
    pick = np.zeros((2 * S, 4 * QUARTER), np.float32)
    for a in range(2):
        for u in range(H):
            pick[S - 1 - (2 * u + a), a * QUARTER + u * H] = 1
            pick[S + 2 * u + a, (2 + a) * QUARTER + u * H + H - 1] = 1
    return pick


def cap_selector():
    pick = np.zeros((4 * S, 8 * 128), np.float32)
    for wx in range(4):
        for v in range(H):
            x = 2 * v + wx - 1
            top = 128 + 0 if x < 0 else 128 + 3 if x >= S else x
            low = 128 + 1 if x < 0 else 128 + 2 if x >= S else S + S - 1 - x
            pick[top, wx * 128 + v] = 1
            pick[low, (4 + wx) * 128 + 96 + v] = 1
    return pick


def tap_selector():
    pick = np.zeros((C * TAPS, C * TAPS), np.float32)
    for i in range(C):
        for tap in range(TAPS):
            pick[i * TAPS + tap, tap * C + i] = 1
    return pick


def down_selector(n_chan):
    local = C // n_chan
    pick = np.zeros((n_chan, local * 4, C * 4), np.float32)
    for i in range(C):
        for ab in range(4):
            pick[i // local, (i % local) * 4 + ab, ab * C + i] = 1
    return pick


def dot(a, b):
    return jnp.dot(a, b, preferred_element_type=F32)


def dot_nt(a, b):
    return lax.dot_general(a, b, (((1,), (1,)), ((), ())), preferred_element_type=F32)


def split_dot_nt(a, selector):
    high = a.astype(BF16)
    rest = a - high.astype(F32)
    middle = rest.astype(BF16)
    low = (rest - middle.astype(F32)).astype(BF16)
    rows = a.shape[0]
    moved = dot_nt(jnp.concatenate([high, middle, low], axis=0), selector)
    return moved[:rows] + moved[rows : 2 * rows] + moved[2 * rows :]


def greet(n_tile, n_chan, me_t, me_c):
    barrier = pltpu.get_barrier_semaphore()
    for k in range(1, n_tile):
        peer = lax.rem(me_t + k, n_tile)
        pl.semaphore_signal(barrier, inc=1, device_id=(peer, me_c), device_id_type=MESH)
    for k in range(1, n_chan):
        peer = lax.rem(me_c + k, n_chan)
        pl.semaphore_signal(barrier, inc=1, device_id=(me_t, peer), device_id_type=MESH)


def remote(src, dst, send_sem, recv_sem, device):
    copy = pltpu.make_async_remote_copy(
        src_ref=src,
        dst_ref=dst,
        send_sem=send_sem,
        recv_sem=recv_sem,
        device_id=device,
        device_id_type=MESH,
    )
    copy.start()
    return copy


def find_owners(table, groups, tiles, wanted):
    def step(s, found):
        for t in range(tiles):
            value = table[s, t, 0]
            found = tuple(jnp.where(value == w, s, f) for w, f in zip(wanted, found))
        return found

    return lax.fori_loop(0, groups, step, (jnp.int32(0),) * len(wanted))


def widen_weights(taps, wide):
    none = jnp.zeros((C, C), F32)
    for a in range(2):
        for b in range(2):
            pieces = []
            for wy in range(4):
                for wx in range(4):
                    dy, dx = wy - a, wx - b
                    if 0 <= dy < 3 and 0 <= dx < 3:
                        tap = 3 * dy + dx
                        pieces.append(taps[:, tap * C : tap * C + C])
                    else:
                        pieces.append(none)
            row = (a * 2 + b) * C
            wide[row : row + C, :] = jnp.concatenate(pieces, axis=1).astype(BF16)


def fill_window(phase, sides, caps, window, t):
    lane = lax.broadcasted_iota(jnp.int32, (C, QUARTER), 1)
    first_col = lax.rem(lane, H) == 0
    last_col = lax.rem(lane, H) == H - 1
    lane_cap = lax.broadcasted_iota(jnp.int32, (C, 128), 1)
    for a in range(2):
        even, odd = phase[a * 2], phase[a * 2 + 1]
        west = jnp.where(
            first_col, sides[:, a * QUARTER : (a + 1) * QUARTER], pltpu.roll(odd, 1, 1)
        )
        east = jnp.where(
            last_col,
            sides[:, (2 + a) * QUARTER : (3 + a) * QUARTER],
            pltpu.roll(even, QUARTER - 1, 1),
        )
        for wx, middle in enumerate((west, even, odd, east)):
            row = ((1 + a) * 4 + wx) * C
            window[t, row : row + C, :] = middle.astype(BF16)
            if a == 1:
                moved = pltpu.roll(middle, H, 1)
                cap = caps[:, wx * 128 : wx * 128 + 128]
                head = jnp.where(lane_cap < H, cap, moved[:, :128])
                moved = jnp.concatenate([head, moved[:, 128:]], axis=1)
                row = wx * C
            else:
                moved = pltpu.roll(middle, QUARTER - H, 1)
                cap = caps[:, (4 + wx) * 128 : (5 + wx) * 128]
                tail = jnp.where(lane_cap >= 128 - H, cap, moved[:, QUARTER - 128 :])
                moved = jnp.concatenate([moved[:, : QUARTER - 128], tail], axis=1)
                row = (12 + wx) * C
            window[t, row : row + C, :] = moved.astype(BF16)


def level_kernel(
    n_tile,
    n_chan,
    tiles,
    feat_hbm,
    cot_hbm,
    cw_hbm,
    dw_hbm,
    rim_sel_hbm,
    half_sel_hbm,
    phase_sel_hbm,
    side_sel_hbm,
    cap_sel_hbm,
    tap_sel_hbm,
    down_sel_hbm,
    cb_smem,
    el_smem,
    et_smem,
    cl_smem,
    ct_smem,
    slot_smem,
    coarse_out,
    grads_out,
    feat,
    cot,
    rim_sel,
    half_sel,
    phase_sel,
    side_sel,
    cap_sel,
    tap_sel,
    down_sel,
    feat_all,
    cw_all,
    dw_all,
    cb_all,
    table_all,
    table,
    rims,
    halos,
    halo_all,
    slots,
    cot_send,
    cot_recv,
    cot_group,
    cot_all,
    wide,
    phases,
    window,
    slope,
    hidden,
    quarter,
    quarter_group,
    quarter_send,
    quarter_recv,
    pack,
    pack_send,
    pack_recv,
    pieces,
    pieces_recv,
    local_sem,
    chan_send,
    chan_recv,
    tile_send,
    tile_recv,
    rim_send,
    rim_recv,
):
    me_t = lax.axis_index("tile")
    me_c = lax.axis_index("chan")
    per = tiles // n_chan
    local = feat.shape[1]
    n_outer = n_tile // 2
    outer, inner = me_t // 2, lax.rem(me_t, 2)

    greet(n_tile, n_chan, me_t, me_c)

    def fetch(src, dst, k):
        copy = pltpu.make_async_copy(src, dst, local_sem.at[k])
        copy.start()
        return copy

    get_feat = fetch(feat_hbm, feat, 0)
    get_rim_sel = fetch(rim_sel_hbm, rim_sel, 1)
    get_cot = fetch(cot_hbm, cot, 2)
    get_half_sel = fetch(half_sel_hbm, half_sel, 3)
    get_own = [
        fetch(cw_hbm, cw_all.at[me_c], 5),
        fetch(dw_hbm, dw_all.at[me_c], 6),
        fetch(feat_hbm.at[pl.ds(me_c * per, per)], feat_all.at[me_c], 4),
        fetch(phase_sel_hbm, phase_sel, 8),
        fetch(side_sel_hbm, side_sel, 9),
        fetch(cap_sel_hbm, cap_sel, 10),
        fetch(tap_sel_hbm, tap_sel, 11),
        fetch(down_sel_hbm, down_sel, 12),
    ]
    row = lax.broadcasted_iota(jnp.int32, (local, 128), 0)
    bias = jnp.zeros((local, 128), F32)
    for n in range(local):
        bias = jnp.where(row == n, cb_smem[n], bias)
    cb_all[pl.ds(me_c, 1)] = bias[None]
    row = lax.broadcasted_iota(jnp.int32, (tiles, 128), 0)
    own_slots = jnp.zeros((tiles, 128), jnp.int32)
    for t in range(tiles):
        own_slots = jnp.where(row == t, slot_smem[0, t], own_slots)
    table_all[pl.ds(me_t, 1)] = own_slots[None]

    pl.semaphore_wait(pltpu.get_barrier_semaphore(), n_tile - 1 + n_chan - 1)

    def to_tiles(kind, src, dst):
        copies = []
        for k in range(1, n_tile):
            d = lax.rem(me_t + k, n_tile)
            copies.append(
                remote(
                    src(d), dst, tile_send.at[kind, k], tile_recv.at[kind, k], (d, me_c)
                )
            )
        return copies

    def to_chans(kind, src, dst):
        copies = []
        for k in range(1, n_chan):
            c = lax.rem(me_c + k, n_chan)
            copies.append(
                remote(
                    src(c), dst, chan_send.at[kind, k], chan_recv.at[kind, k], (me_t, c)
                )
            )
        return copies

    def finish(copies):
        for copy in copies:
            copy.wait()

    def chan_rows(c):
        return pl.ds(pl.multiple_of(c * local, local), local)

    table_copies = to_tiles(0, lambda d: table_all.at[me_t], table_all.at[me_t])
    small_copies = (
        to_chans(1, lambda c: cw_hbm, cw_all.at[me_c])
        + to_chans(2, lambda c: dw_hbm, dw_all.at[me_c])
        + to_chans(3, lambda c: cb_all.at[me_c], cb_all.at[me_c])
    )
    feat_copies = [
        to_chans(FEAT + t, lambda c: feat_hbm.at[c * per + t], feat_all.at[me_c, t])
        for t in range(per)
    ]

    get_feat.wait()
    get_rim_sel.wait()
    pixels = feat[...].reshape(tiles * local, S * S)
    my_rims = dot(pixels, rim_sel[...]).astype(BF16)
    rims[pl.ds(me_t, 1)] = my_rims.reshape(1, tiles, local, 4 * S)
    across = outer * 2 + 1 - inner
    forwards = [
        remote(
            rims.at[me_t], rims.at[me_t], rim_send.at[1, 0], rim_recv.at[1, 0], (across, me_c)
        )
    ]
    straight = []
    for k in range(1, n_outer):
        d = lax.rem(outer + k, n_outer) * 2 + inner
        straight.append(
            remote(rims.at[me_t], rims.at[me_t], rim_send.at[0, k], rim_recv.at[0, k], (d, me_c))
        )

    get_cot.wait()
    get_half_sel.wait()
    coarse_tiles = cot.shape[0]
    cots = cot[...].reshape(coarse_tiles * local, S * S)
    chunks = [cots[:, 256 * j : 256 * j + 256] for j in range(16)]
    moved = dot(jnp.concatenate(chunks, axis=0), half_sel[...]).astype(BF16)
    for j in range(16):
        lanes = slice((j % 8) * 128, (j % 8) * 128 + 128)
        for n in range(coarse_tiles):
            first = (j * coarse_tiles + n) * local
            rows = moved[first : first + local]
            slots[n * 4 + (j // 8) * 2, :, lanes] = rows[:, :128]
            slots[n * 4 + (j // 8) * 2 + 1, :, lanes] = rows[:, 128:]

    finish(table_copies)
    to_smem = pltpu.make_async_copy(table_all, table, local_sem.at[7])
    to_smem.start()
    to_smem.wait()
    homes = find_owners(table, n_tile, tiles, tuple(me_t * tiles + m for m in range(tiles)))
    owners = [slot_smem[0, t] // tiles for t in range(tiles)]
    for d in range(n_tile):
        chosen = jnp.int32(0)
        for m in range(tiles):
            chosen = jnp.where(homes[m] == d, m, chosen)
        cot_send[d] = slots[chosen]
    cot_recv[pl.ds(me_t, 1)] = cot_send[pl.ds(me_t, 1)]

    for k in range(1, n_outer):
        straight[k - 1].wait_recv()
        source = lax.rem(outer + n_outer - k, n_outer) * 2 + inner
        forwards.append(
            remote(
                rims.at[source],
                rims.at[source],
                rim_send.at[1, k],
                rim_recv.at[1, k],
                (across, me_c),
            )
        )
    cot_copies = to_tiles(1, lambda d: cot_send.at[d], cot_recv.at[me_t])

    finish(get_own)
    finish(small_copies)
    widen_weights(dot(cw_all[...].reshape(C, C * TAPS), tap_sel[...]), wide)
    down = jnp.zeros((C, 4 * C), F32)
    for c in range(n_chan):
        down = down + dot(dw_all[c], down_sel[c])
    down_t = down.T.astype(BF16)
    down = down.astype(BF16)

    def deinterleave(t):
        finish(feat_copies[t])
        pixels = feat_all[:, t].reshape(C, S * S)
        chunks = [pixels[:, 512 * j : 512 * j + 512] for j in range(8)]
        moved = dot(jnp.concatenate(chunks, axis=0), phase_sel[...])
        for j in range(8):
            rows = moved[j * C : (j + 1) * C]
            for p in range(4):
                phases[t, p, :, 128 * j : 128 * j + 128] = rows[:, p * 128 : p * 128 + 128]

    deinterleave(0)
    finish(forwards)
    for copy in straight:
        copy.wait_send()
    lane = lax.broadcasted_iota(jnp.int32, (local, 128), 1)
    for t in range(tiles):
        def half_of(link, rim):
            block = rims[link // tiles, lax.rem(link, tiles)].astype(F32)
            return jnp.where(rim >= 2, block[:, 128:], block[:, :128])

        strips = []
        corners = jnp.zeros((local, 128), F32)
        for k, place in enumerate((0, 0, 1, 1)):
            rim = lax.rem(k + 2 + et_smem[k, t], 4)
            held = half_of(el_smem[k, t], rim)
            strips.append(jnp.where(lax.rem(rim, 2) == place, held, pltpu.roll(held, S, 1)))
            link = cl_smem[k, t]
            rim = lax.rem(k + 3 + ct_smem[k, t], 4)
            held = half_of(jnp.maximum(link, 0), rim)
            near, far = held if k == 0 else pltpu.roll(held, k, 1), pltpu.roll(held, S + k, 1)
            value = jnp.where(lax.rem(rim, 2) == 0, near, far)
            value = jnp.where(link >= 0, value, jnp.zeros_like(value))
            corners = jnp.where(lane == k, value, corners)
        north, west, south, east = strips
        west_east = jnp.where(lane < S, west, east)
        north_south = jnp.where(lane < S, north, south)
        halos[t] = jnp.concatenate([west_east, north_south, corners], axis=1).astype(BF16)
    halo_all[pl.ds(me_c, 1)] = halos[pl.ds(me_c * per, per)][None]
    halo_copies = to_chans(4, lambda c: halos.at[pl.ds(c * per, per)], halo_all.at[me_c])

    for t in range(1, per):
        deinterleave(t)
    finish(halo_copies)
    bias = jnp.concatenate([cb_all[...].reshape(C, 128)[:, :1]] * 4, axis=0)
    def forward_cotangent():
        finish(cot_copies)
        for t in range(tiles):
            cot_group[t] = cot_recv[owners[t]]
        cot_all[pl.ds(me_c, 1)] = cot_group[pl.ds(me_c * per, per)][None]
        return to_chans(
            6, lambda c: cot_group.at[pl.ds(c * per, per)], cot_all.at[me_c]
        )

    quarter_copies = []
    halo = jnp.concatenate([halo_all[:, t].reshape(C, 6 * S) for t in range(per)], axis=0)
    sides = dot(halo[:, : 2 * S], side_sel[...])
    caps = dot(halo[:, 2 * S :], cap_sel[...])
    for t in range(per):
        rows = slice(t * C, (t + 1) * C)
        fill_window([phases[t, p] for p in range(4)], sides[rows], caps[rows], window, t)
        pre = dot(wide[...], window[t]) + bias
        squashed = 1.0 / (1.0 + jnp.exp(-pre))
        slope[t] = squashed * (1.0 + pre * (1.0 - squashed))
        hidden[t] = (pre * squashed).astype(BF16)
        quarter[t] = dot(down, hidden[t]).astype(BF16)
        quarter_group[pl.ds(me_c, 1), t] = quarter[t, chan_rows(me_c)][None]
        quarter_copies += to_chans(
            FEAT + per + t, lambda c: quarter.at[t, chan_rows(c)], quarter_group.at[me_c, t]
        )
        if t == 0:
            cot_chan_copies = forward_cotangent()

    def forward_quarters():
        finish(quarter_copies)
        for d in range(n_tile):
            chosen = jnp.int32(0)
            for t in range(tiles):
                chosen = jnp.where(owners[t] == d, t, chosen)
            quarter_send[d] = quarter_group[chosen // per, lax.rem(chosen, per)]
        quarter_recv[pl.ds(me_t, 1)] = quarter_send[pl.ds(me_t, 1)]
        return to_tiles(2, lambda d: quarter_send.at[d], quarter_recv.at[me_t])

    quarter_moves = forward_quarters()
    finish(cot_chan_copies)
    grad_wide = jnp.zeros((4 * C, 16 * C), F32)
    grad_down = jnp.zeros((C, 4 * C), F32)
    grad_bias = jnp.zeros((8, 4 * C), F32)
    ones = jnp.ones((8, QUARTER), BF16)
    for t in range(per):
        back = cot_all[:, t].reshape(C, QUARTER)
        grad_pre = (dot(down_t, back) * slope[t]).astype(BF16)
        grad_down = grad_down + dot_nt(back, hidden[t])
        grad_bias = grad_bias + dot_nt(ones, grad_pre)
        grad_wide = grad_wide + dot_nt(grad_pre, window[t])
    taps = []
    for dy in range(3):
        for dx in range(3):
            total = jnp.zeros((C, C), F32)
            for a in range(2):
                for b in range(2):
                    row = (a * 2 + b) * C
                    col = ((a + dy) * 4 + b + dx) * C
                    total = total + grad_wide[row : row + C, col : col + C]
            taps.append(total)
    moved = split_dot_nt(jnp.concatenate(taps, axis=1), tap_sel[...])
    pack[:, : TAPS * C] = moved
    pack[:, TAPS * C :] = jnp.zeros((C, PACK - TAPS * C), F32)
    grad_down = split_dot_nt(grad_down, down_sel[...].reshape(4 * C, 4 * C))
    total = grad_bias[:1, :C]
    for ab in range(1, 4):
        total = total + grad_bias[:1, ab * C : ab * C + C]
    for c in range(n_chan):
        rows = slice(c * local, c * local + local)
        pack[c * local : c * local + 1, BIAS_COL : BIAS_COL + local] = total[:, rows]
        wide_cols = slice(c * 4 * local, (c + 1) * 4 * local)
        for n in range(C // local):
            col = DOWN_COL + n * 4 * local
            pack[rows, col : col + 4 * local] = grad_down[n * local : (n + 1) * local, wide_cols]

    def join_quarters():
        finish(quarter_moves)
        placed = [quarter_recv[home] for home in homes]
        chunks = []
        for n in range(coarse_tiles):
            for j in range(16):
                lanes = slice((j % 8) * 128, (j % 8) * 128 + 128)
                q = n * 4 + (j // 8) * 2
                chunks.append(jnp.concatenate([placed[q][:, lanes], placed[q + 1][:, lanes]], 1))
        moved = dot_nt(jnp.concatenate(chunks, axis=0), half_sel[...]).astype(BF16)
        for n in range(coarse_tiles):
            for j in range(16):
                first = (n * 16 + j) * local
                coarse_out[n, :, 256 * j : 256 * j + 256] = moved[first : first + local]

    pack_send[...] = pack[:, :PACK_USED].astype(BF16)
    pack_recv[pl.ds(me_c, 1)] = pack_send[chan_rows(me_c)][None]
    finish(to_chans(7, lambda c: pack_send.at[chan_rows(c)], pack_recv.at[me_c]))
    total = pack_recv[0].astype(F32)
    for c in range(1, n_chan):
        total = total + pack_recv[c].astype(F32)
    total = jnp.concatenate([total, jnp.zeros((local, PACK - PACK_USED), F32)], axis=1)
    n_pieces = PACK // 128
    if n_tile == n_pieces:
        for n in range(n_pieces):
            pieces[n] = total[:, n * 128 : n * 128 + 128]
        pieces_recv[pl.ds(me_t, 1)] = pieces[pl.ds(me_t, 1)]
        piece_copies = to_tiles(3, lambda d: pieces.at[d], pieces_recv.at[me_t])
        join_quarters()
        finish(piece_copies)
        total = pieces_recv[0]
        for s in range(1, n_tile):
            total = total + pieces_recv[s]
        grads_out[pl.ds(me_t, 1)] = total[None]
        finish(to_tiles(4, lambda d: grads_out.at[me_t], grads_out.at[me_t]))
    else:
        pieces[pl.ds(me_t, 1)] = total[None]
        piece_copies = to_tiles(3, lambda d: pieces.at[me_t], pieces.at[me_t])
        join_quarters()
        finish(piece_copies)
        total = pieces[0]
        for s in range(1, n_tile):
            total = total + pieces[s]
        for n in range(n_pieces):
            grads_out[n] = total[:, n * 128 : n * 128 + 128]


def finish_kernel(joined, grads, coarse, grad_conv, grad_bias, grad_down):
    local = coarse.shape[1]
    coarse[...] = joined[...]
    whole = jnp.concatenate([grads[n] for n in range(grads.shape[0])], axis=1)
    grad_conv[...] = whole[:, : TAPS * C]
    grad_bias[...] = whole[:1, BIAS_COL : BIAS_COL + local]
    for n in range(C // local):
        col = DOWN_COL + n * 4 * local
        grad_down[n * local : (n + 1) * local] = whole[:, col : col + 4 * local]


def on_device(
    n_tile,
    n_chan,
    features,
    conv_weight,
    conv_bias,
    down_weight,
    cotangent,
    edge_links,
    edge_turns,
    corner_links,
    corner_turns,
    child_slot,
):
    tiles, local = features.shape[0], features.shape[1]
    per = tiles // n_chan
    n_pieces = PACK // 128
    hbm = pl.BlockSpec(memory_space=pltpu.HBM)
    vmem = pl.BlockSpec(memory_space=pltpu.VMEM)
    smem = pl.BlockSpec(memory_space=pltpu.SMEM)
    tables = [edge_links.T, edge_turns.T, corner_links.T, corner_turns.T, child_slot[None]]

    def const(values):
        return jnp.asarray(values, BF16)

    half = half_selector()
    selectors = [
        const(rim_selector()),
        const(half),
        const(phase_selector()),
        const(side_selector()),
        const(cap_selector()),
        const(tap_selector()),
        const(down_selector(n_chan)),
    ]
    split = n_tile == n_pieces
    piece_shape = (n_tile, local, 128 if split else PACK)
    dma = pltpu.SemaphoreType.DMA
    joined, grads = pl.pallas_call(
        functools.partial(level_kernel, n_tile, n_chan, tiles),
        out_shape=[
            jax.ShapeDtypeStruct(cotangent.shape, BF16),
            jax.ShapeDtypeStruct((n_pieces, local, 128), F32),
        ],
        in_specs=[hbm] * 11 + [smem] * 6,
        out_specs=[vmem] * 2,
        scratch_shapes=[
            pltpu.VMEM(features.shape, BF16),
            pltpu.VMEM(cotangent.shape, BF16),
        ]
        + [pltpu.VMEM(selector.shape, BF16) for selector in selectors]
        + [
            pltpu.VMEM((n_chan, per, local, S * S), BF16),
            pltpu.VMEM((n_chan, local, C * TAPS), BF16),
            pltpu.VMEM((n_chan, C, local * 4), BF16),
            pltpu.VMEM((n_chan, local, 128), F32),
            pltpu.VMEM((n_tile, tiles, 128), jnp.int32),
            pltpu.SMEM((n_tile, tiles, 128), jnp.int32),
            pltpu.VMEM((n_tile, tiles, local, 4 * S), BF16),
            pltpu.VMEM((tiles, local, 6 * S), BF16),
            pltpu.VMEM((n_chan, per, local, 6 * S), BF16),
            pltpu.VMEM((tiles, local, QUARTER), BF16),
            pltpu.VMEM((n_tile, local, QUARTER), BF16),
            pltpu.VMEM((n_tile, local, QUARTER), BF16),
            pltpu.VMEM((tiles, local, QUARTER), BF16),
            pltpu.VMEM((n_chan, per, local, QUARTER), BF16),
            pltpu.VMEM((4 * C, 16 * C), BF16),
            pltpu.VMEM((per, 4, C, QUARTER), F32),
            pltpu.VMEM((per, 16 * C, QUARTER), BF16),
            pltpu.VMEM((per, 4 * C, QUARTER), F32),
            pltpu.VMEM((per, 4 * C, QUARTER), BF16),
            pltpu.VMEM((per, C, QUARTER), BF16),
            pltpu.VMEM((n_chan, per, local, QUARTER), BF16),
            pltpu.VMEM((n_tile, local, QUARTER), BF16),
            pltpu.VMEM((n_tile, local, QUARTER), BF16),
            pltpu.VMEM((C, PACK), F32),
            pltpu.VMEM((C, PACK_USED), BF16),
            pltpu.VMEM((n_chan, local, PACK_USED), BF16),
            pltpu.VMEM(piece_shape, F32),
            pltpu.VMEM((n_tile, local, 128), F32),
            dma((13,)),
            dma((FEAT + 2 * per, n_chan)),
            dma((FEAT + 2 * per, n_chan)),
            dma((5, n_tile)),
            dma((5, n_tile)),
            dma((2, n_tile // 2)),
            dma((2, n_tile // 2)),
        ],
        compiler_params=pltpu.CompilerParams(
            collective_id=0, has_side_effects=True, vmem_limit_bytes=VMEM_LIMIT
        ),
        name="unet_level",
    )(features, cotangent, conv_weight, down_weight, *selectors, conv_bias, *tables)
    coarse, grad_conv, grad_bias, grad_down = pl.pallas_call(
        finish_kernel,
        out_shape=[
            jax.ShapeDtypeStruct(cotangent.shape, BF16),
            jax.ShapeDtypeStruct(conv_weight.shape, F32),
            jax.ShapeDtypeStruct((1, local), F32),
            jax.ShapeDtypeStruct(down_weight.shape, F32),
        ],
        in_specs=[vmem] * 2,
        out_specs=[vmem] * 4,
        compiler_params=pltpu.CompilerParams(vmem_limit_bytes=VMEM_LIMIT),
        name="finish",
    )(joined, grads)
    return (coarse, grad_conv, grad_bias.reshape(local), grad_down)


def solution(mesh):
    n_tile, n_chan = mesh.shape["tile"], mesh.shape["chan"]
    in_specs = (
        P("tile", "chan", None),
        P("chan", None),
        P("chan"),
        P(None, "chan"),
        P("tile", "chan", None),
        P("tile", None),
        P("tile", None),
        P("tile", None),
        P("tile", None),
        P("tile"),
    )
    out_specs = (P("tile", "chan", None), P("chan", None), P("chan"), P(None, "chan"))
    return jax.shard_map(
        functools.partial(on_device, n_tile, n_chan),
        mesh=mesh,
        in_specs=in_specs,
        out_specs=out_specs,
        check_vma=False,
    )
```
